128 devices in a mesh: tm: 32 (over z, y, core), rows: 4 (over x).
Axes of the slice: x: 4, y: 4, z: 4, core: 2. Of those that a mesh axis runs over, the one named last changes fastest.
Arguments:
- inputs: bfloat16 [64, 32, 80, 256], P('tm', 'rows'), may hold values from -64 to 64
- cotangent: bfloat16 [64, 32, 80, 256], P('tm', 'rows'), may hold values from -64 to 64
- gain_one: float32 [256], replicated, may hold values from 0.1 to 1.9
- gain_two: float32 [256], replicated, may hold values from 0.1 to 1.9
- weight_one: bfloat16 [6912, 256], replicated, may hold values from -4 to 4
- weight_two: bfloat16 [6912, 256], replicated, may hold values from -4 to 4
- first_one: float32 [1769472], P(('tm', 'rows')), may hold values from -6 to 6
- second_one: float32 [1769472], P(('tm', 'rows')), may hold values from 1 to 10
- first_two: float32 [1769472], P(('tm', 'rows')), may hold values from -6 to 6
- second_two: float32 [1769472], P(('tm', 'rows')), may hold values from 1 to 10
Outputs:
- input_grad: bfloat16 [64, 32, 80, 256], P('tm', 'rows')
- new_weight_one: bfloat16 [6912, 256], replicated
- new_weight_two: bfloat16 [6912, 256], replicated
- new_first_one: float32 [1769472], P(('tm', 'rows'))
- new_second_one: float32 [1769472], P(('tm', 'rows'))
- new_first_two: float32 [1769472], P(('tm', 'rows'))
- new_second_two: float32 [1769472], P(('tm', 'rows'))
The draws below stay inside these ranges and needn't reach their ends.
All inputs are finite; a program needn't handle non-finite values.
Results may differ from the reference program's by a relative error of at most 0.018.
Values may be sent and summed in bfloat16 or wider, within the bound.
No kernel may reach another device: no remote copies, remote signals or barrier semaphores. Data moves between devices by JAX's collectives and lax.ppermute only.
A program may use at most 128 MiB of HBM per device.

```python
import math
import jax
import jax.numpy as jnp
from jax import lax

C = 256
GROUPS = 32
WIDTH = 80
FRAMES = 64
HEIGHT = 32
PARAMS = 1769472


def ramp_scales(key, slope):
    key_channel, key_row = jax.random.split(key)
    channel_scale = jnp.exp(jax.random.uniform(key_channel, (C,), jnp.float32, math.log(0.3), math.log(3.0)))
    row_scale = jnp.exp(jax.random.uniform(key_row, (HEIGHT, 1, 1), jnp.float32, math.log(0.7), math.log(1.4)))
    position = jnp.arange(FRAMES, dtype=jnp.float32) / max(FRAMES - 1, 1)
    frame_scale = 2.0 + slope * (2.0 * position - 1.0)
    return frame_scale[:, None, None, None] * row_scale[None] * channel_scale


def draw_inputs(key, part):
    key = jax.random.fold_in(key, 11)
    key_scale, key_noise = jax.random.split(key)
    scales = ramp_scales(key_scale, 1.0)
    noise = jnp.clip(jax.random.normal(key_noise, (FRAMES, HEIGHT, WIDTH, C), jnp.float32), -5.0, 5.0)
    return (noise * scales).astype(jnp.bfloat16)


def draw_cotangent(key, part):
    key = jax.random.fold_in(key, 23)
    key_scale, key_noise = jax.random.split(key)
    scales = ramp_scales(key_scale, -1.0)
    noise = jnp.clip(jax.random.normal(key_noise, (FRAMES, HEIGHT, WIDTH, C), jnp.float32), -5.0, 5.0)
    return (noise * scales).astype(jnp.bfloat16)


def block_scale(stream_key, extent, cuts, least, largest):
    gain = 1.0
    for axis_at, parts in cuts:
        draws = jax.random.uniform(jax.random.fold_in(jax.random.fold_in(stream_key, 6), axis_at), (parts,), jnp.float32, least / len(cuts), largest / len(cuts))
        gain = gain * jnp.repeat(jnp.exp(draws), extent[axis_at] // parts).reshape((-1,) + (1,) * (len(extent) - 1 - axis_at))
    return gain


def centred(rng, dims, width, bound, cuts=(), kind=jnp.bfloat16):
    entries = jax.random.normal(rng, dims, jnp.float32) * width
    if len(cuts) > 0:
        entries = block_scale(rng, dims, cuts, -0.22, 0.18) * entries
    return jnp.clip(entries, min=-bound, max=bound).astype(kind)


def setup_inputs(seed: int = 0) -> dict:
    keys = jax.random.split(jax.random.key(seed), 11)
    return {
        "inputs": draw_inputs(jax.random.fold_in(keys[10], 71), 0),
        "cotangent": draw_cotangent(jax.random.fold_in(keys[10], 71), 0),
        "gain_one": jnp.clip(1.0 + 0.18 * jax.random.normal(keys[2], (C,), jnp.float32), 0.1, 1.9),
        "gain_two": jnp.clip(1.0 + 0.18 * jax.random.normal(keys[3], (C,), jnp.float32), 0.1, 1.9),
        "weight_one": centred(keys[4], (27 * C, C), 1.0, 4.0),
        "weight_two": centred(keys[5], (27 * C, C), 1.0, 4.0),
        "first_one": centred(keys[6], (PARAMS,), 1.0, 6.0, ((0, 128),), jnp.float32),
        "second_one": jnp.clip(jnp.exp(math.log(10.0) - 2.3025851 * jax.random.uniform(keys[7], (PARAMS,), jnp.float32) ** block_scale(keys[7], (PARAMS,), ((0, 128),), -0.2, 0.2)), 1.0, 10.0),
        "first_two": centred(keys[8], (PARAMS,), 1.0, 6.0, ((0, 128),), jnp.float32),
        "second_two": jnp.clip(jnp.exp(math.log(10.0) - 2.3025851 * jax.random.uniform(keys[9], (PARAMS,), jnp.float32) ** block_scale(keys[9], (PARAMS,), ((0, 128),), -0.2, 0.2)), 1.0, 10.0),
    }


norm_eps = 1e-05
learn_rate = 0.25
beta_one = 0.9
beta_two = 0.95
decay_rate = 0.1
adam_eps = 1e-08
first_fix = 1.0 - 0.9 ** 10
second_fix = 1.0 - 0.95 ** 10

def group_mean(values):
    channels = values.shape[-1]
    per_channel = lax.optimization_barrier(jnp.mean(values.reshape(-1, channels), axis=0))
    return jnp.repeat(lax.optimization_barrier(jnp.mean(per_channel.reshape(GROUPS, -1), axis=1)), channels // GROUPS)

def normalize(values):
    centered = values - group_mean(values)
    inverse = lax.rsqrt(group_mean(centered * centered) + norm_eps)
    return (centered * inverse, inverse)

def conv_forward(hidden, weight):
    frames, height, columns, channels = hidden.shape
    padded = jnp.pad(hidden, ((2, 0), (1, 1), (1, 1), (0, 0)))
    taps = weight.reshape(27, channels, channels)
    summed_taps = jnp.zeros((frames * height * columns, channels), jnp.float32)
    for tap_index in range(27):
        time_off, row_off, col_off = (tap_index // 9, tap_index // 3 % 3, tap_index % 3)
        sliced = padded[time_off:time_off + frames, row_off:row_off + height, col_off:col_off + columns].reshape(-1, channels)
        summed_taps = summed_taps + jnp.dot(sliced, taps[tap_index], preferred_element_type=jnp.float32)
    return (summed_taps * (27.0 * channels) ** (-0.5)).reshape(hidden.shape)

def conv_backward(grad, weight):
    frames, height, columns, channels = grad.shape
    padded = jnp.pad(grad, ((0, 2), (1, 1), (1, 1), (0, 0)))
    taps = weight.reshape(27, channels, channels)
    summed_taps = jnp.zeros((frames * height * columns, channels), jnp.float32)
    for tap_index in range(27):
        time_off, row_off, col_off = (2 - tap_index // 9, 2 - tap_index // 3 % 3, 2 - tap_index % 3)
        sliced = padded[time_off:time_off + frames, row_off:row_off + height, col_off:col_off + columns].reshape(-1, channels)
        summed_taps = summed_taps + jnp.dot(sliced, taps[tap_index].T, preferred_element_type=jnp.float32)
    return (summed_taps * (27.0 * channels) ** (-0.5)).reshape(grad.shape)

def weight_grad(hidden, grad):
    frames, height, columns, channels = hidden.shape
    padded = jnp.pad(hidden, ((2, 0), (1, 1), (1, 1), (0, 0)))
    grad_rows = grad.reshape(-1, channels)
    blocks = []
    for tap_index in range(27):
        time_off, row_off, col_off = (tap_index // 9, tap_index // 3 % 3, tap_index % 3)
        sliced = padded[time_off:time_off + frames, row_off:row_off + height, col_off:col_off + columns].reshape(-1, channels)
        blocks.append(jnp.dot(sliced.T, grad_rows, preferred_element_type=jnp.float32))
    return jnp.concatenate(blocks, axis=0) * (27.0 * channels) ** (-0.5)

def adamw_step(weight, grad, first, second):
    gradient = grad.reshape(-1)
    first_new = beta_one * first + (1.0 - beta_one) * gradient
    second_new = beta_two * second + (1.0 - beta_two) * gradient * gradient
    old_values = weight.reshape(-1).astype(jnp.float32)
    updated = old_values * (1.0 - learn_rate * decay_rate) - learn_rate * (first_new / first_fix) / (jnp.sqrt(second_new / second_fix) + adam_eps)
    return (updated.astype(jnp.bfloat16).reshape(weight.shape), first_new, second_new)

def reference(inputs, cotangent, gain_one, gain_two, weight_one, weight_two, first_one, second_one, first_two, second_two):
    in_val = inputs.astype(jnp.float32)
    in_hat, inv_one = normalize(in_val)
    pre_one = in_hat * gain_one
    gate_one = jax.nn.sigmoid(pre_one)
    hidden_one = (pre_one * gate_one).astype(jnp.bfloat16)
    middle = conv_forward(hidden_one, weight_one).astype(jnp.bfloat16)
    mid_hat, inv_two = normalize(middle.astype(jnp.float32))
    pre_two = mid_hat * gain_two
    gate_two = jax.nn.sigmoid(pre_two)
    hidden_two = (pre_two * gate_two).astype(jnp.bfloat16)
    grad_two = weight_grad(hidden_two, cotangent)
    back_two = conv_backward(cotangent, weight_two)
    slope_two = back_two * gate_two * (1.0 + pre_two * (1.0 - gate_two)) * gain_two
    mid_grad = (inv_two * (slope_two - group_mean(slope_two) - mid_hat * group_mean(slope_two * mid_hat))).astype(jnp.bfloat16)
    grad_one = weight_grad(hidden_one, mid_grad)
    back_one = conv_backward(mid_grad, weight_one)
    slope_one = back_one * gate_one * (1.0 + pre_one * (1.0 - gate_one)) * gain_one
    input_grad = (cotangent.astype(jnp.float32) + inv_one * (slope_one - group_mean(slope_one) - in_hat * group_mean(slope_one * in_hat))).astype(jnp.bfloat16)
    new_weight_one, new_first_one, new_second_one = adamw_step(weight_one, grad_one, first_one, second_one)
    new_weight_two, new_first_two, new_second_two = adamw_step(weight_two, grad_two, first_two, second_two)
    return (input_grad, new_weight_one, new_weight_two, new_first_one, new_second_one, new_first_two, new_second_two)
```

```python
import jax
import jax.numpy as jnp
from jax import lax
from jax.sharding import PartitionSpec as P

GROUPS = 32


norm_eps = 1e-05
learn_rate = 0.25
beta_one = 0.9
beta_two = 0.95
decay_rate = 0.1
adam_eps = 1e-08
first_fix = 1.0 - 0.9**10
second_fix = 1.0 - 0.95**10


def shifted(value, axis, steps):
    count = lax.axis_size(axis)
    leading, last = (max(0, -steps), min(count, count - steps))
    return lax.ppermute(value, axis, [(source, source + steps) for source in range(leading, last)])


def with_halo(array, sides, width):
    for axis, dim in sides:
        count, length = (lax.axis_size(axis), array.shape[dim])
        up = [(i, (i + 1) % count) for i in range(count - 1)]
        down = [(j, i) for i, j in up]
        last = lax.slice_in_dim(array, length - width, length, axis=dim)
        leading = lax.slice_in_dim(array, 0, width, axis=dim)
        before = lax.ppermute(last, axis, up)
        after = lax.ppermute(leading, axis, down)
        array = jnp.concatenate([before, array, after], axis=dim)
    return array


def coordinates(index):
    return (index >> 5, index >> 3 & 3, index >> 2 & 1, index & 3)


def flat_index(z, y, core, x):
    return ((z * 4 + y) * 2 + core) * 4 + x


CHIP_GROUPS = [
    [flat_index(z, y, core, x) for z in range(4) for y in range(4) for x in range(4)]
    for core in range(2)
]
CORE_PAIRS = [(i, i ^ 4) for i in range(128)]
BOTH = ("tm", "rows")


def from_everyone(first, second):
    row = jnp.concatenate([first, second, jnp.zeros((64,), jnp.float32)])
    spread = jnp.broadcast_to(row[None], (128, 128))
    arrived = lax.all_to_all(spread, BOTH, 0, 0, tiled=True)
    return arrived[:, :GROUPS], arrived[:, GROUPS : 2 * GROUPS]


def per_group(values):
    channels = values.shape[-1]
    per_channel = jnp.sum(values.reshape(-1, channels), axis=0)
    return jnp.sum(per_channel.reshape(GROUPS, -1), axis=1)


def broaden(statistic, channels):
    return jnp.repeat(statistic, channels // GROUPS)


def normalize(values, cell_count):
    channels = values.shape[-1]
    here_count = cell_count / 128.0
    here_mean = per_group(values) / here_count
    centered = values - broaden(here_mean, channels)
    means, squares = from_everyone(here_mean, per_group(centered * centered))
    center = jnp.mean(means, axis=0)
    offsets = means - center
    spread = jnp.sum(squares, axis=0) + here_count * jnp.sum(offsets * offsets, axis=0)
    inverse_wide = broaden(lax.rsqrt(spread / cell_count + norm_eps), channels)
    center_wide = broaden(center, channels)
    return center_wide, inverse_wide


def norm_backward(slope, normed, inverse_wide, cell_count):
    channels = slope.shape[-1]
    means, crosses = from_everyone(per_group(slope), per_group(slope * normed))
    mean_sum, cross_sum = jnp.sum(means, axis=0), jnp.sum(crosses, axis=0)
    return inverse_wide * (
        slope
        - broaden(mean_sum / cell_count, channels)
        - normed * broaden(cross_sum / cell_count, channels)
    )


def extend(volume, upcoming):
    edge_frames = volume if upcoming else volume
    arrived = shifted(edge_frames, "tm", -1 if upcoming else 1)
    joined = jnp.concatenate((volume, arrived) if upcoming else (arrived, volume), axis=0)
    rimmed = with_halo(joined, (("rows", 1),), 1)
    return jnp.pad(rimmed, ((0, 0), (0, 0), (1, 1), (0, 0)))


def patches(extended, backward, frames, rows_here, columns):
    pieces = []
    for tap_index in range(27):
        time_off, row_off, col_off = (tap_index // 9, tap_index // 3 % 3, tap_index % 3)
        if backward:
            time_off, row_off, col_off = (2 - time_off, 2 - row_off, 2 - col_off)
        pieces.append(
            extended[
                time_off : time_off + frames,
                row_off : row_off + rows_here,
                col_off : col_off + columns,
            ]
        )
    return jnp.concatenate(pieces, axis=-1).reshape(frames * rows_here * columns, -1)


def flipped(weight, channels):
    return (
        weight.reshape(27, channels, channels).transpose(0, 2, 1).reshape(27 * channels, channels)
    )


def reduce_grad(local_grad):
    core = lax.axis_index("tm") % 2
    halves = local_grad.astype(jnp.bfloat16).reshape(16, 2, 216, 256)
    kept = lax.dynamic_index_in_dim(halves, core, 1, keepdims=False)
    given = lax.dynamic_index_in_dim(halves, 1 - core, 1, keepdims=False)
    taken = lax.ppermute(given, BOTH, CORE_PAIRS)
    pair_sum = (kept.astype(jnp.float32) + taken.astype(jnp.float32)).astype(jnp.bfloat16)
    arrived = lax.all_to_all(
        pair_sum.reshape(64, 54, 256), BOTH, 0, 0, axis_index_groups=CHIP_GROUPS, tiled=True
    )
    return jnp.sum(arrived.astype(jnp.float32), axis=0).reshape(-1)


def gather_weights(part_one, part_two):
    core = lax.axis_index("tm") % 2
    both = jnp.concatenate([part_one.reshape(54, 256), part_two.reshape(54, 256)], axis=0)
    spread = jnp.broadcast_to(both[None], (64, 108, 256))
    own = lax.all_to_all(spread, BOTH, 0, 0, axis_index_groups=CHIP_GROUPS, tiled=True)
    other = lax.ppermute(own, BOTH, CORE_PAIRS)
    low = jnp.where(core == 0, own, other).reshape(16, 1, 4, 108, 256)
    high = jnp.where(core == 0, other, own).reshape(16, 1, 4, 108, 256)
    whole = jnp.concatenate([low, high], axis=1)
    return (whole[:, :, :, :54].reshape(6912, 256), whole[:, :, :, 54:].reshape(6912, 256))


def adamw_share(weight, gradient, first, second):
    share_len = first.shape[0]
    own_share = lax.dynamic_slice_in_dim(
        weight.reshape(-1), lax.axis_index(("tm", "rows")) * share_len, share_len
    ).astype(jnp.float32)
    first_new = beta_one * first + (1.0 - beta_one) * gradient
    second_new = beta_two * second + (1.0 - beta_two) * gradient * gradient
    updated = own_share * (1.0 - learn_rate * decay_rate) - learn_rate * (first_new / first_fix) / (
        jnp.sqrt(second_new / second_fix) + adam_eps
    )
    return (updated.astype(jnp.bfloat16), first_new, second_new)


def local(
    inputs,
    cotangent,
    gain_one,
    gain_two,
    weight_one,
    weight_two,
    first_one,
    second_one,
    first_two,
    second_two,
):
    frames, rows_here, columns, channels = inputs.shape
    cell_count = float(
        frames
        * rows_here
        * columns
        * lax.axis_size("tm")
        * lax.axis_size("rows")
        * (channels // GROUPS)
    )
    conv_scale = (27.0 * channels) ** (-0.5)
    in_val = inputs.astype(jnp.float32)
    center_one, inv_one = normalize(in_val, cell_count)
    in_hat = (in_val - center_one) * inv_one
    pre_one = in_hat * gain_one
    gate_one = jax.nn.sigmoid(pre_one)
    hidden_one = (pre_one * gate_one).astype(jnp.bfloat16)
    patch_one = patches(extend(hidden_one, False), False, frames, rows_here, columns)
    middle = (
        jnp.dot(patch_one, weight_one, preferred_element_type=jnp.float32) * conv_scale
    ).astype(jnp.bfloat16)
    mid_val = middle.astype(jnp.float32).reshape(inputs.shape)
    center_two, inv_two = normalize(mid_val, cell_count)
    mid_hat = (mid_val - center_two) * inv_two
    pre_two = mid_hat * gain_two
    gate_two = jax.nn.sigmoid(pre_two)
    hidden_two = (pre_two * gate_two).astype(jnp.bfloat16)
    patch_two = patches(extend(hidden_two, False), False, frames, rows_here, columns)
    grad_two = (
        lax.dot_general(
            patch_two,
            cotangent.reshape(-1, channels),
            (((0,), (0,)), ((), ())),
            preferred_element_type=jnp.float32,
        )
        * conv_scale
    )
    share_two = reduce_grad(grad_two)
    patch_back = patches(extend(cotangent, True), True, frames, rows_here, columns)
    back_two = (
        jnp.dot(patch_back, flipped(weight_two, channels), preferred_element_type=jnp.float32)
        * conv_scale
    ).reshape(inputs.shape)
    slope_two = back_two * gate_two * (1.0 + pre_two * (1.0 - gate_two)) * gain_two
    mid_grad = norm_backward(slope_two, mid_hat, inv_two, cell_count).astype(jnp.bfloat16)
    grad_one = (
        lax.dot_general(
            patch_one,
            mid_grad.reshape(-1, channels),
            (((0,), (0,)), ((), ())),
            preferred_element_type=jnp.float32,
        )
        * conv_scale
    )
    share_one = reduce_grad(grad_one)
    patch_mid = patches(extend(mid_grad, True), True, frames, rows_here, columns)
    back_one = (
        jnp.dot(patch_mid, flipped(weight_one, channels), preferred_element_type=jnp.float32)
        * conv_scale
    ).reshape(inputs.shape)
    slope_one = back_one * gate_one * (1.0 + pre_one * (1.0 - gate_one)) * gain_one
    input_grad = (
        cotangent.astype(jnp.float32) + norm_backward(slope_one, in_hat, inv_one, cell_count)
    ).astype(jnp.bfloat16)
    part_one, new_first_one, new_second_one = adamw_share(
        weight_one, share_one, first_one, second_one
    )
    part_two, new_first_two, new_second_two = adamw_share(
        weight_two, share_two, first_two, second_two
    )
    new_weight_one, new_weight_two = gather_weights(part_one, part_two)
    return (
        input_grad,
        new_weight_one,
        new_weight_two,
        new_first_one,
        new_second_one,
        new_first_two,
        new_second_two,
    )


def solution(mesh):
    return jax.shard_map(
        local,
        mesh=mesh,
        in_specs=(
            P("tm", "rows", None, None),
            P("tm", "rows", None, None),
            P(),
            P(),
            P(),
            P(),
            P(("tm", "rows")),
            P(("tm", "rows")),
            P(("tm", "rows")),
            P(("tm", "rows")),
        ),
        out_specs=(
            P("tm", "rows", None, None),
            P(),
            P(),
            P(("tm", "rows")),
            P(("tm", "rows")),
            P(("tm", "rows")),
            P(("tm", "rows")),
        ),
        check_vma=False,
    )
```

```python
import jax
import jax.numpy as jnp
from jax import lax
from jax.experimental import pallas as pl
from jax.experimental.pallas import tpu as pltpu
from jax.sharding import PartitionSpec as P

C = 256
COLS = 80
ROWS = 8
FR = 2
CELLS = FR * ROWS * COLS
EXT = (FR + 2) * (ROWS + 2) * COLS
BAND = ROWS * COLS
norm_eps = 1e-05
F32 = jnp.float32
BF16 = jnp.bfloat16
HERE = float(CELLS * 8)
TOTAL = HERE * 128.0
SCALE = (27.0 * C) ** (-0.5)
SHARE = 108
PIECE = 112
BLOCK = 432
BOTH = ("tm", "rows")
CORE_PAIRS = [(i, i ^ 4) for i in range(128)]
CHIP_GROUPS = [
    [((z * 4 + y) * 2 + core) * 4 + x for z in range(4) for y in range(4) for x in range(4)]
    for core in range(2)
]
learn_rate = 0.25
beta_one = 0.9
beta_two = 0.95
decay_rate = 0.1
adam_eps = 1e-08
first_fix = 1.0 - 0.9**10
second_fix = 1.0 - 0.95**10


def mixed(value, matrix):
    return jnp.dot(value, matrix, precision=lax.Precision.HIGHEST, preferred_element_type=F32)


def iotas(shape):
    return lax.broadcasted_iota(jnp.int32, shape, 0), lax.broadcasted_iota(jnp.int32, shape, 1)


def spread_matrix(offset):
    lane, channel = iotas((128, C))
    return jnp.where(lane == (channel >> 3) + offset, 1.0, 0.0).astype(F32)


def pack_row(first, second):
    channel, lane = iotas((C, 128))
    head = jnp.where((channel >> 3) == lane, 1.0, 0.0).astype(F32)
    tail = jnp.where((channel >> 3) + 32 == lane, 1.0, 0.0).astype(F32)
    wide = jnp.broadcast_to(first, (8, C)), jnp.broadcast_to(second, (8, C))
    row = mixed(wide[0], head) + mixed(wide[1], tail)
    return jnp.broadcast_to(row[0:1], (128, 128))


def read_norm(table):
    total = jnp.sum(table, axis=0, keepdims=True)
    center = total / 128.0
    offset = table - center
    square = jnp.sum(offset * offset, axis=0, keepdims=True)
    low, high = spread_matrix(0), spread_matrix(32)
    wide = lambda v, m: mixed(jnp.broadcast_to(v, (8, 128)), m)[0:1]
    spread = wide(total, high) + HERE * wide(square, low)
    return wide(center, low), lax.rsqrt(spread / TOTAL + norm_eps)


def read_sums(table):
    total = jnp.sum(table, axis=0, keepdims=True) / TOTAL
    wide = lambda m: mixed(jnp.broadcast_to(total, (8, 128)), m)[0:1]
    return wide(spread_matrix(0)), wide(spread_matrix(32))


def folded(values):
    return jnp.sum(values.reshape(-1, 8, C), axis=0)


def chunk(index, size=COLS):
    return pl.ds(pl.multiple_of(index * size, size), size)


def local_moments(read, count):
    zero = jnp.zeros((8, C), F32)
    sums = lax.fori_loop(0, count, lambda i, s: s + folded(read(i)), zero)
    ch_sum = jnp.sum(sums, axis=0, keepdims=True)
    r, c = iotas((C, C))
    same = jnp.where((r >> 3) == (c >> 3), 1.0, 0.0).astype(F32)
    mean = mixed(jnp.broadcast_to(ch_sum, (8, C)), same)[0:1] / HERE

    def squares(i, s):
        off = read(i) - mean
        return s + folded(off * off)

    ch_sq = jnp.sum(lax.fori_loop(0, count, squares, zero), axis=0, keepdims=True)
    return pack_row(mean / 8.0, ch_sq)


def store_shifted(target, rows, value, backward):
    col = lax.broadcasted_iota(jnp.int32, value.shape, 0)
    left = jnp.where(col == 0, 0.0, pltpu.roll(value, 1, 0))
    right = jnp.where(col == COLS - 1, 0.0, pltpu.roll(value, COLS - 1, 0))
    one, three = (right, left) if backward else (left, right)
    target[rows, 0:C] = one.astype(BF16)
    target[rows, C : 2 * C] = value.astype(BF16)
    target[rows, 2 * C : 3 * C] = three.astype(BF16)


def each_row(own, frames, above, below, ok, upcoming, target, make, backward):
    own_at, halo_at = (0, FR) if upcoming else (FR, 0)

    def body(source, at, flag):
        def step(i, _):
            frame, row = at + i // ROWS, i % ROWS
            value = make(source[chunk(i), :].astype(F32))
            if flag is not None:
                value = value * flag
            store_shifted(target, chunk(frame * (ROWS + 2) + row + 1), value, backward)
            return 0

        lax.fori_loop(0, FR * ROWS, step, 0)

    body(own, own_at, None)
    body(frames, halo_at, ok[0])

    def edge(i, _):
        flag = jnp.where((i < FR) == (halo_at == 0), ok[0], 1.0)
        top = make(above[chunk(i), :].astype(F32)) * (flag * ok[1])
        store_shifted(target, chunk(i * (ROWS + 2)), top, backward)
        low = make(below[chunk(i), :].astype(F32)) * (flag * ok[2])
        store_shifted(target, chunk(i * (ROWS + 2) + ROWS + 1), low, backward)
        return 0

    lax.fori_loop(0, FR + 2, edge, 0)


def conv(patches, weight, write, backward):
    for t in range(FR):
        total = None
        for a in range(3):
            for b in range(3):
                f, r = (t + 2 - a, 2 - b) if backward else (t + a, b)
                at = (f * (ROWS + 2) + r) * COLS
                left = patches[at : at + BAND, :]
                tap = (9 * a + 3 * b) * C
                if backward:
                    right = jnp.concatenate([weight[tap + k * C : tap + (k + 1) * C, :] for k in range(3)], axis=1)
                    part = lax.dot_general(left, right, (((1,), (1,)), ((), ())), preferred_element_type=F32)
                else:
                    part = jnp.dot(left, weight[tap : tap + 3 * C, :], preferred_element_type=F32)
                total = part if total is None else total + part
        write(t, total * SCALE)


def wgrad(patches, grad, whole):
    for a in range(3):
        for b in range(3):
            total = None
            for t in range(FR):
                at = ((t + a) * (ROWS + 2) + b) * COLS
                part = lax.dot_general(
                    patches[at : at + BAND, :],
                    grad[t * BAND : (t + 1) * BAND, :],
                    (((0,), (0,)), ((), ())),
                    preferred_element_type=F32,
                )
                total = part if total is None else total + part
            tap = (9 * a + 3 * b) * C
            whole[tap : tap + 3 * C, :] = total * SCALE


def cut_pieces(whole, core, flat, kept, given):
    flat[...] = jnp.zeros_like(flat)

    def block(i, _):
        for side, out in ((core, kept), (1 - core, given)):
            at = pl.multiple_of(i * BLOCK + side * (BLOCK // 2), 8)
            slab = whole[pl.ds(at, BLOCK // 2), :]
            flat[pl.ds(0, BLOCK // 2, 2), :] = slab[:, :128]
            flat[pl.ds(1, BLOCK // 2, 2), :] = slab[:, 128:]
            for x in range(4):
                out[i * 4 + x] = flat[x * SHARE : x * SHARE + PIECE, :].astype(BF16)
        return 0

    lax.fori_loop(0, 16, block, 0)


def silu_parts(value, center, inverse, gain):
    hat = (value - center) * inverse
    pre = hat * gain
    return hat, pre, jax.nn.sigmoid(pre)


def stats_kernel(inputs, row):
    row[...] = local_moments(lambda i: inputs[chunk(i), :].astype(F32), FR * ROWS)


def conv_kernel(ok, inputs, frames, above, below, table, gain, weight, patches, middle, row):
    center, inverse = read_norm(table[...])

    def hidden(value):
        _, pre, gate = silu_parts(value, center, inverse, gain[...])
        return pre * gate

    each_row(inputs, frames, above, below, ok, False, patches, hidden, False)

    def write(t, value):
        middle[t * BAND : (t + 1) * BAND, :] = value.astype(BF16)

    conv(patches, weight, write, False)
    row[...] = local_moments(lambda i: middle[chunk(i), :].astype(F32), FR * ROWS)


def back_two_kernel(ok, cotangent, frames, above, below, weight, back, patches):
    each_row(cotangent, frames, above, below, ok, True, patches, lambda v: v, True)

    def write(t, value):
        back[t * BAND : (t + 1) * BAND, :] = value

    conv(patches, weight, write, True)


def slopes(read, back, center, inverse, gain, slope):
    def step(i, sums):
        hat, pre, gate = silu_parts(read(i), center, inverse, gain)
        here = back[chunk(i), :] * gate * (1.0 + pre * (1.0 - gate)) * gain
        slope[chunk(i), :] = here
        return sums[0] + folded(here), sums[1] + folded(here * hat)

    zero = jnp.zeros((8, C), F32)
    plain, cross = lax.fori_loop(0, FR * ROWS, step, (zero, zero))
    return pack_row(jnp.sum(plain, axis=0, keepdims=True), jnp.sum(cross, axis=0, keepdims=True))


def slope_kernel(middle, table, gain, back, slope, row):
    center, inverse = read_norm(table[...])
    read = lambda i: middle[chunk(i), :].astype(F32)
    row[...] = slopes(read, back, center, inverse, gain[...], slope)


def grad_two_kernel(ok, core, middle, frames, above, below, table, gain, cotangent, kept, given, patches, whole, flat):
    center, inverse = read_norm(table[...])

    def hidden(value):
        _, pre, gate = silu_parts(value, center, inverse, gain[...])
        return pre * gate

    each_row(middle, frames, above, below, ok, False, patches, hidden, False)
    wgrad(patches, cotangent, whole)
    cut_pieces(whole, core[0], flat, kept, given)


def grad_one_kernel(core, slope, middle, table, sums, patches, mid_grad, kept, given, whole, flat):
    center, inverse = read_norm(table[...])
    mean, cross = read_sums(sums[...])

    def step(i, _):
        hat = (middle[chunk(i), :].astype(F32) - center) * inverse
        mid_grad[chunk(i), :] = (inverse * (slope[chunk(i), :] - mean - hat * cross)).astype(BF16)
        return 0

    lax.fori_loop(0, FR * ROWS, step, 0)
    wgrad(patches, mid_grad, whole)
    cut_pieces(whole, core[0], flat, kept, given)


def back_one_kernel(ok, mid_grad, frames, above, below, weight, inputs, table, gain, slope, row, patches, back):
    each_row(mid_grad, frames, above, below, ok, True, patches, lambda v: v, True)

    def write(t, value):
        back[t * BAND : (t + 1) * BAND, :] = value

    conv(patches, weight, write, True)
    center, inverse = read_norm(table[...])
    read = lambda i: inputs[chunk(i), :].astype(F32)
    row[...] = slopes(read, back, center, inverse, gain[...], slope)


def final_kernel(slope, inputs, table, sums, cotangent, result):
    center, inverse = read_norm(table[...])
    mean, cross = read_sums(sums[...])

    def step(i, _):
        hat = (inputs[chunk(i), :].astype(F32) - center) * inverse
        grad = inverse * (slope[chunk(i), :] - mean - hat * cross)
        result[chunk(i), :] = (cotangent[chunk(i), :].astype(F32) + grad).astype(BF16)
        return 0

    lax.fori_loop(0, FR * ROWS, step, 0)


def adam_kernel(arrived, own, first, second, first_new, second_new, spread):
    add = lambda i, s: s + arrived[i].astype(F32)
    gradient = lax.fori_loop(0, 64, add, jnp.zeros((PIECE, 128), F32))[:SHARE]
    one = beta_one * first[...] + (1.0 - beta_one) * gradient
    two = beta_two * second[...] + (1.0 - beta_two) * gradient * gradient
    first_new[...] = one
    second_new[...] = two
    updated = own[...].astype(F32) * (1.0 - learn_rate * decay_rate) - learn_rate * (one / first_fix) / (
        jnp.sqrt(two / second_fix) + adam_eps
    )
    piece = jnp.concatenate([updated, jnp.zeros((PIECE - SHARE, 128), F32)], axis=0).astype(BF16)

    def copy(i, _):
        spread[i] = piece
        return 0

    lax.fori_loop(0, 64, copy, 0)


def assemble_kernel(core, own, other, weight, flat):
    def fill(low, high):
        def block(i, _):
            for s in range(8):
                piece = (low if s < 4 else high)[i * 4 + s % 4]
                flat[s * SHARE : s * SHARE + PIECE, :] = piece.astype(F32)
            rows = pl.ds(pl.multiple_of(i * BLOCK, BLOCK), BLOCK)
            weight[rows, 0:128] = flat[pl.ds(0, BLOCK, 2), :].astype(BF16)
            weight[rows, 128:256] = flat[pl.ds(1, BLOCK, 2), :].astype(BF16)
            return 0

        lax.fori_loop(0, 16, block, 0)

    @pl.when(core[0] == 0)
    def _():
        fill(own, other)

    @pl.when(core[0] != 0)
    def _():
        fill(other, own)


def run(kernel, scalars, arrays, outs, scratch=(), mib=24, flops=0):
    vmem = pl.BlockSpec(memory_space=pltpu.VMEM)
    size = sum(x.size * x.dtype.itemsize for x in (*arrays, *outs))
    return pl.pallas_call(
        kernel,
        out_shape=tuple(outs),
        in_specs=[pl.BlockSpec(memory_space=pltpu.SMEM)] * len(scalars) + [vmem] * len(arrays),
        out_specs=tuple(vmem for _ in outs),
        scratch_shapes=list(scratch),
        compiler_params=pltpu.CompilerParams(vmem_limit_bytes=mib * 1024 * 1024),
        cost_estimate=pl.CostEstimate(flops=flops, bytes_accessed=size, transcendentals=0),
    )(*scalars, *arrays)


def everyone(row):
    return lax.all_to_all(row, BOTH, 0, 0, tiled=True)


def halo(block, upcoming):
    steps, bands = lax.axis_size("tm"), lax.axis_size("rows")
    forward = [(i, i + 1) for i in range(steps - 1)]
    backward = [(j, i) for i, j in forward]
    frames = lax.ppermute(block, "tm", backward if upcoming else forward)
    pair = lambda r: (block[:, r], frames[:, r]) if upcoming else (frames[:, r], block[:, r])
    down = [(i, i + 1) for i in range(bands - 1)]
    up = [(j, i) for i, j in down]
    above = lax.ppermute(jnp.concatenate(pair(ROWS - 1), axis=0), "rows", down)
    below = lax.ppermute(jnp.concatenate(pair(0), axis=0), "rows", up)
    return frames.reshape(CELLS, C), above.reshape(-1, C), below.reshape(-1, C)


def cells(array):
    return array.reshape(FR, ROWS, COLS, C)


def scatter_sum(kept, given):
    taken = lax.ppermute(given, BOTH, CORE_PAIRS)
    pair_sum = (kept.astype(F32) + taken.astype(F32)).astype(BF16)
    return lax.all_to_all(pair_sum, BOTH, 0, 0, axis_index_groups=CHIP_GROUPS, tiled=True)


def own_share(weight):
    place = lax.axis_index(BOTH) * (SHARE // 2)
    return lax.dynamic_slice_in_dim(weight, place, SHARE // 2, axis=0).reshape(SHARE, 128)


def local(
    inputs,
    cotangent,
    gain_one,
    gain_two,
    weight_one,
    weight_two,
    first_one,
    second_one,
    first_two,
    second_two,
):
    shape = jax.ShapeDtypeStruct
    step, band = lax.axis_index("tm"), lax.axis_index("rows")
    core = (step % 2).astype(jnp.int32).reshape(1)
    inside = lambda *tests: jnp.stack([jnp.where(t, 1.0, 0.0).astype(F32) for t in tests])
    above_ok, below_ok = band > 0, band < lax.axis_size("rows") - 1
    ok_before = inside(step > 0, above_ok, below_ok)
    ok_after = inside(step < lax.axis_size("tm") - 1, above_ok, below_ok)
    gain_one, gain_two = gain_one.reshape(1, C), gain_two.reshape(1, C)
    flat_inputs, flat_cot = inputs.reshape(CELLS, C), cotangent.reshape(CELLS, C)

    row_type = shape((128, 128), F32)
    act_type, wide_type = shape((CELLS, C), BF16), shape((CELLS, C), F32)
    patch_type = shape((EXT, 3 * C), BF16)
    piece_type = shape((64, PIECE, 128), BF16)
    moment_type = shape((SHARE, 128), F32)
    patch_scratch = pltpu.VMEM((EXT, 3 * C), BF16)
    whole_scratch = pltpu.VMEM((27 * C, C), F32)
    flat_scratch = pltpu.VMEM((BLOCK + 8, 128), F32)
    work = 2 * CELLS * 27 * C * C

    (row_one,) = run(stats_kernel, (), (flat_inputs,), (row_type,))
    table_one = everyone(row_one)
    halo_in = halo(inputs, False)
    halo_cot = halo(cotangent, True)
    (back_two,) = run(
        back_two_kernel, (ok_after,), (flat_cot, *halo_cot, weight_two), (wide_type,), (patch_scratch,), flops=work
    )
    patch_one, middle, row_two = run(
        conv_kernel,
        (ok_before,),
        (flat_inputs, *halo_in, table_one, gain_one, weight_one),
        (patch_type, act_type, row_type),
        flops=work,
    )
    table_two = everyone(row_two)
    halo_mid = halo(cells(middle), False)
    slope_two, row_three = run(
        slope_kernel, (), (middle, table_two, gain_two, back_two), (wide_type, row_type)
    )
    table_three = everyone(row_three)
    kept_two, given_two = run(
        grad_two_kernel,
        (ok_before, core),
        (middle, *halo_mid, table_two, gain_two, flat_cot),
        (piece_type, piece_type),
        (patch_scratch, whole_scratch, flat_scratch),
        flops=work,
    )
    mid_grad, kept_one, given_one = run(
        grad_one_kernel,
        (core,),
        (slope_two, middle, table_two, table_three, patch_one),
        (act_type, piece_type, piece_type),
        (whole_scratch, flat_scratch),
        flops=work,
    )
    arrived_two = scatter_sum(kept_two, given_two)
    arrived_one = scatter_sum(kept_one, given_one)
    halo_grad = halo(cells(mid_grad), True)
    slope_one, row_four = run(
        back_one_kernel,
        (ok_after,),
        (mid_grad, *halo_grad, weight_one, flat_inputs, table_one, gain_one),
        (wide_type, row_type),
        (patch_scratch, pltpu.VMEM((CELLS, C), F32)),
        flops=work,
    )
    table_four = everyone(row_four)
    (input_grad,) = run(
        final_kernel, (), (slope_one, flat_inputs, table_one, table_four, flat_cot), (act_type,)
    )

    def update(arrived, weight, first, second):
        first_new, second_new, spread = run(
            adam_kernel,
            (),
            (arrived, own_share(weight), first.reshape(SHARE, 128), second.reshape(SHARE, 128)),
            (moment_type, moment_type, piece_type),
        )
        own = lax.all_to_all(spread, BOTH, 0, 0, axis_index_groups=CHIP_GROUPS, tiled=True)
        other = lax.ppermute(own, BOTH, CORE_PAIRS)
        (whole,) = run(
            assemble_kernel,
            (core,),
            (own, other),
            (shape((27 * C, C), BF16),),
            (pltpu.VMEM((2 * BLOCK + 8, 128), F32),),
        )
        return whole, first_new.reshape(-1), second_new.reshape(-1)

    new_weight_two, new_first_two, new_second_two = update(arrived_two, weight_two, first_two, second_two)
    new_weight_one, new_first_one, new_second_one = update(arrived_one, weight_one, first_one, second_one)
    return (
        cells(input_grad),
        new_weight_one,
        new_weight_two,
        new_first_one,
        new_second_one,
        new_first_two,
        new_second_two,
    )


def solution(mesh):
    split, share = P("tm", "rows", None, None), P(("tm", "rows"))
    return jax.shard_map(
        local,
        mesh=mesh,
        in_specs=(split, split, P(), P(), P(), P(), share, share, share, share),
        out_specs=(split, P(), P(), share, share, share, share),
        check_vma=False,
    )
```

```python
import jax
import jax.numpy as jnp
from jax import lax
from jax.experimental import pallas as pl
from jax.experimental.pallas import tpu as pltpu
from jax.sharding import PartitionSpec as P

C = 256
COLS = 80
ROWS = 8
FR = 2
CELLS = FR * ROWS * COLS
EXT = (FR + 2) * (ROWS + 2) * COLS
BAND = ROWS * COLS
norm_eps = 1e-05
F32 = jnp.float32
BF16 = jnp.bfloat16
HERE = float(CELLS * 8)
TOTAL = HERE * 128.0
SCALE = (27.0 * C) ** (-0.5)
SHARE = 108
PIECE = 112
BLOCK = 432
BOTH = ("tm", "rows")
CORE_PAIRS = [(i, i ^ 4) for i in range(128)]
CHIP_GROUPS = [
    [((z * 4 + y) * 2 + core) * 4 + x for z in range(4) for y in range(4) for x in range(4)]
    for core in range(2)
]
learn_rate = 0.25
beta_one = 0.9
beta_two = 0.95
decay_rate = 0.1
adam_eps = 1e-08
first_fix = 1.0 - 0.9**10
second_fix = 1.0 - 0.95**10


def mixed(value, matrix):
    return jnp.dot(value, matrix, precision=lax.Precision.HIGHEST, preferred_element_type=F32)


def iotas(shape):
    return lax.broadcasted_iota(jnp.int32, shape, 0), lax.broadcasted_iota(jnp.int32, shape, 1)


def spread_matrix(offset):
    lane, channel = iotas((128, C))
    return jnp.where(lane == (channel >> 3) + offset, 1.0, 0.0).astype(F32)


def pack_row(first, second):
    channel, lane = iotas((C, 128))
    head = jnp.where((channel >> 3) == lane, 1.0, 0.0).astype(F32)
    tail = jnp.where((channel >> 3) + 32 == lane, 1.0, 0.0).astype(F32)
    wide = jnp.broadcast_to(first, (8, C)), jnp.broadcast_to(second, (8, C))
    row = mixed(wide[0], head) + mixed(wide[1], tail)
    return jnp.broadcast_to(row[0:1], (128, 128))


def read_norm(table):
    total = jnp.sum(table, axis=0, keepdims=True)
    center = total / 128.0
    offset = table - center
    square = jnp.sum(offset * offset, axis=0, keepdims=True)
    low, high = spread_matrix(0), spread_matrix(32)
    wide = lambda v, m: mixed(jnp.broadcast_to(v, (8, 128)), m)[0:1]
    spread = wide(total, high) + HERE * wide(square, low)
    return wide(center, low), lax.rsqrt(spread / TOTAL + norm_eps)


def read_sums(table):
    total = jnp.sum(table, axis=0, keepdims=True) / TOTAL
    wide = lambda m: mixed(jnp.broadcast_to(total, (8, 128)), m)[0:1]
    return wide(spread_matrix(0)), wide(spread_matrix(32))


def folded(values):
    return jnp.sum(values.reshape(-1, 8, C), axis=0)


def chunk(index, size=COLS):
    return pl.ds(pl.multiple_of(index * size, size), size)


def local_moments(read, count):
    zero = jnp.zeros((8, C), F32)
    sums = lax.fori_loop(0, count, lambda i, s: s + folded(read(i)), zero)
    ch_sum = jnp.sum(sums, axis=0, keepdims=True)
    r, c = iotas((C, C))
    same = jnp.where((r >> 3) == (c >> 3), 1.0, 0.0).astype(F32)
    mean = mixed(jnp.broadcast_to(ch_sum, (8, C)), same)[0:1] / HERE

    def squares(i, s):
        off = read(i) - mean
        return s + folded(off * off)

    ch_sq = jnp.sum(lax.fori_loop(0, count, squares, zero), axis=0, keepdims=True)
    return pack_row(mean / 8.0, ch_sq)


def store_shifted(target, rows, value, backward):
    col = lax.broadcasted_iota(jnp.int32, value.shape, 0)
    left = jnp.where(col == 0, 0.0, pltpu.roll(value, 1, 0))
    right = jnp.where(col == COLS - 1, 0.0, pltpu.roll(value, COLS - 1, 0))
    one, three = (right, left) if backward else (left, right)
    target[rows, 0:C] = one.astype(BF16)
    target[rows, C : 2 * C] = value.astype(BF16)
    target[rows, 2 * C : 3 * C] = three.astype(BF16)


def each_row(own, above, below, frames, ok, upcoming, target, make, backward):
    own_at, halo_at = (0, FR) if upcoming else (FR, 0)

    def put(source, i, frame, row, flag):
        value = make(source[chunk(i), :].astype(F32))
        if flag is not None:
            value = value * flag
        store_shifted(target, chunk(frame * (ROWS + 2) + row), value, backward)

    def inner(i, _):
        put(own, i, own_at + i // ROWS, i % ROWS + 1, None)
        return 0

    def edge(i, _):
        put(above, i, own_at + i, 0, ok[1])
        put(below, i, own_at + i, ROWS + 1, ok[2])
        return 0

    def outer(i, _):
        row = i % (ROWS + 2)
        flag = ok[0] * jnp.where(row == 0, ok[1], jnp.where(row == ROWS + 1, ok[2], 1.0))
        put(frames, i, halo_at + i // (ROWS + 2), row, flag)
        return 0

    lax.fori_loop(0, FR * ROWS, inner, 0)
    lax.fori_loop(0, FR, edge, 0)
    lax.fori_loop(0, FR * (ROWS + 2), outer, 0)


def conv(patches, weight, write, backward):
    for t in range(FR):
        total = None
        for a in range(3):
            for b in range(3):
                f, r = (t + 2 - a, 2 - b) if backward else (t + a, b)
                at = (f * (ROWS + 2) + r) * COLS
                left = patches[at : at + BAND, :]
                tap = (9 * a + 3 * b) * C
                if backward:
                    right = jnp.concatenate([weight[tap + k * C : tap + (k + 1) * C, :] for k in range(3)], axis=1)
                    part = lax.dot_general(left, right, (((1,), (1,)), ((), ())), preferred_element_type=F32)
                else:
                    part = jnp.dot(left, weight[tap : tap + 3 * C, :], preferred_element_type=F32)
                total = part if total is None else total + part
        write(t, total * SCALE)


def both_frames(patches, place):
    starts = [(f * (ROWS + 2) + r) * COLS for f, r in map(place, range(FR))]
    return jnp.concatenate([patches[at : at + BAND, :] for at in starts], axis=0)


def wgrad(patches, grad, whole):
    for a in range(3):
        ready = patches.get(a + FR - 1)
        for b in range(3):
            left = both_frames(ready, lambda t: (t + a, b))
            total = lax.dot_general(
                left, grad[...], (((0,), (0,)), ((), ())), preferred_element_type=F32
            )
            tap = (9 * a + 3 * b) * C
            whole[tap : tap + 3 * C, :] = total * SCALE


def cut_pieces(whole, core, flat, kept, given):
    flat[...] = jnp.zeros_like(flat)
    for side, out in ((1 - core, given), (core, kept)):

        def block(i, _):
            at = pl.multiple_of(i * BLOCK + side * (BLOCK // 2), 8)
            slab = whole[pl.ds(at, BLOCK // 2), :]
            flat[pl.ds(0, BLOCK // 2, 2), :] = slab[:, :128]
            flat[pl.ds(1, BLOCK // 2, 2), :] = slab[:, 128:]
            for x in range(4):
                out.ref[i * 4 + x] = flat[x * SHARE : x * SHARE + PIECE, :].astype(BF16)
            return 0

        lax.fori_loop(0, 16, block, 0)
        out.send()


def silu_parts(value, center, inverse, gain):
    hat = (value - center) * inverse
    pre = hat * gain
    return hat, pre, jax.nn.sigmoid(pre)


def stats_kernel(inputs, row):
    inputs = inputs.get()
    row.ref[...] = local_moments(lambda i: inputs[chunk(i), :].astype(F32), FR * ROWS)


def conv_kernel(ok, inputs, above, below, frames, table, gain, weight, patches, middle, row):
    center, inverse = read_norm(table.get()[...])
    gain = gain.get()[...]

    def hidden(value):
        _, pre, gate = silu_parts(value, center, inverse, gain)
        return pre * gate

    each_row(inputs.get(), above.get(), below.get(), frames.get(), ok, False, patches.ref, hidden, False)
    patches.send()

    def write(t, value):
        middle.ref[t * BAND : (t + 1) * BAND, :] = value.astype(BF16)

    conv(patches.ref, weight.get(), write, False)
    middle.send()
    row.ref[...] = local_moments(lambda i: middle.ref[chunk(i), :].astype(F32), FR * ROWS)


def slopes(read, back, center, inverse, gain, slope, hidden=None):
    def step(i, sums):
        hat, pre, gate = silu_parts(read(i), center, inverse, gain)
        if hidden is not None:
            hidden[chunk(i), :] = (pre * gate).astype(BF16)
        here = back[chunk(i), :] * gate * (1.0 + pre * (1.0 - gate)) * gain
        slope[chunk(i), :] = here
        return sums[0] + folded(here), sums[1] + folded(here * hat)

    zero = jnp.zeros((8, C), F32)
    plain, cross = lax.fori_loop(0, FR * ROWS, step, (zero, zero))
    return pack_row(jnp.sum(plain, axis=0, keepdims=True), jnp.sum(cross, axis=0, keepdims=True))


def second_kernel(
    ok, core, cotangent, above, below, frames, weight, middle, table, gain, slope, row, kept, given, patches, back, hidden, whole, flat
):
    each_row(cotangent.get(), above.get(), below.get(), frames.get(), ok, True, patches, lambda v: v, True)

    def write(t, value):
        back[t * BAND : (t + 1) * BAND, :] = value

    conv(patches, weight.get(), write, True)
    center, inverse = read_norm(table.get()[...])
    middle = middle.get()
    read = lambda i: middle[chunk(i), :].astype(F32)
    row.ref[...] = slopes(read, back, center, inverse, gain.get()[...], slope.ref, hidden)
    slope.send()
    turned = hidden[...].astype(F32).T.astype(BF16)
    for a in range(3):
        for b in range(3):
            right = both_frames(patches, lambda t: (t + 2 - a, 2 - b))
            total = jnp.dot(turned, right, preferred_element_type=F32)
            total = total * SCALE
            for c in range(3):
                tap = (9 * a + 3 * b + c) * C
                whole[tap : tap + C, :] = total[:, c * C : (c + 1) * C]
    cut_pieces(whole, core[0], flat, kept, given)


def grad_one_kernel(core, slope, middle, patches, table, sums, mid_grad, kept, given, whole, flat):
    center, inverse = read_norm(table.get()[...])
    mean, cross = read_sums(sums.get()[...])
    slope, middle = slope.get(), middle.get()

    def step(i, _):
        hat = (middle[chunk(i), :].astype(F32) - center) * inverse
        mid_grad.ref[chunk(i), :] = (inverse * (slope[chunk(i), :] - mean - hat * cross)).astype(BF16)
        return 0

    lax.fori_loop(0, FR * ROWS, step, 0)
    mid_grad.send()
    wgrad(patches, mid_grad.ref, whole)
    cut_pieces(whole, core[0], flat, kept, given)


def back_one_kernel(ok, mid_grad, above, below, frames, weight, inputs, table, gain, slope, row, patches, back):
    each_row(mid_grad.get(), above.get(), below.get(), frames.get(), ok, True, patches, lambda v: v, True)

    def write(t, value):
        back[t * BAND : (t + 1) * BAND, :] = value

    conv(patches, weight.get(), write, True)
    center, inverse = read_norm(table.get()[...])
    inputs = inputs.get()
    read = lambda i: inputs[chunk(i), :].astype(F32)
    row.ref[...] = slopes(read, back, center, inverse, gain.get()[...], slope.ref)


def final_kernel(slope, inputs, table, sums, cotangent, result):
    center, inverse = read_norm(table.get()[...])
    mean, cross = read_sums(sums.get()[...])
    slope, inputs, cotangent = slope.get(), inputs.get(), cotangent.get()

    def step(i, _):
        hat = (inputs[chunk(i), :].astype(F32) - center) * inverse
        grad = inverse * (slope[chunk(i), :] - mean - hat * cross)
        result.ref[chunk(i), :] = (cotangent[chunk(i), :].astype(F32) + grad).astype(BF16)
        return 0

    lax.fori_loop(0, FR * ROWS, step, 0)


def adam_step(arrived, own, first, second, first_new, second_new):
    gradient = jnp.zeros((PIECE, 128), F32)
    for k in range(4):
        ready = arrived.get(k)
        gradient = lax.fori_loop(16 * k, 16 * k + 16, lambda i, s: s + ready[i].astype(F32), gradient)
    gradient = gradient[:SHARE]
    one = beta_one * first.get()[...] + (1.0 - beta_one) * gradient
    two = beta_two * second.get()[...] + (1.0 - beta_two) * gradient * gradient
    first_new.ref[...] = one
    second_new.ref[...] = two
    updated = own.get()[...].astype(F32) * (1.0 - learn_rate * decay_rate) - learn_rate * (one / first_fix) / (
        jnp.sqrt(two / second_fix) + adam_eps
    )
    return jnp.concatenate([updated, jnp.zeros((PIECE - SHARE, 128), F32)], axis=0).astype(BF16)


def adam_two_kernel(arrived, own, first, second, first_new, second_new, part):
    part.ref[0] = adam_step(arrived, own, first, second, first_new, second_new)


def adam_one_kernel(arrived, own, first, second, first_new, second_new, spread):
    piece = adam_step(arrived, own, first, second, first_new, second_new)

    def copy(i, _):
        spread.ref[i] = piece
        return 0

    for k in range(4):
        lax.fori_loop(16 * k, 16 * k + 16, copy, 0)
        spread.send(k)


def assemble(block, piece, weight, flat):
    for s in range(8):
        flat[s * SHARE : s * SHARE + PIECE, :] = piece(s).astype(F32)
    rows = pl.ds(pl.multiple_of(block * BLOCK, BLOCK), BLOCK)
    weight[rows, 0:128] = flat[pl.ds(0, BLOCK, 2), :].astype(BF16)
    weight[rows, 128:256] = flat[pl.ds(1, BLOCK, 2), :].astype(BF16)


def assemble_kernel(core, own, other, weight, flat, halves, arrive):
    parts = 4
    copies = [
        [
            pltpu.make_async_copy(
                source.at[pl.ds(16 * k, 16)], halves.at[place, pl.ds(16 * k, 16)], arrive.at[n, k]
            )
            for n, (source, place) in enumerate(((own, core[0]), (other, 1 - core[0])))
        ]
        for k in range(parts)
    ]
    for pair in copies:
        for copy in pair:
            copy.start()

    for k in range(parts):
        for copy in copies[k]:
            copy.wait()

        def block(i, _):
            assemble(i, lambda s: halves[s // 4, i * 4 + s % 4], weight.ref, flat)
            return 0

        lax.fori_loop(4 * k, 4 * k + 4, block, 0)
        weight.send(k)


def assemble_all_kernel(gathered, weight, flat):
    for k in range(4):
        ready = gathered.get(k)

        def block(i, _):
            assemble(i, lambda s: ready[i * 8 + s], weight.ref, flat)
            return 0

        lax.fori_loop(4 * k, 4 * k + 4, block, 0)
        weight.send(k)


class Coming:
    def __init__(self, ref, copies=()):
        self.ref, self.copies = ref, list(copies)
        for copy in self.copies:
            copy.start()
        self.parts = len(self.copies)

    def get(self, part=None):
        last = self.parts - 1 if part is None else part
        while self.copies and self.parts - len(self.copies) <= last:
            self.copies.pop(0).wait()
        return self.ref


class Going:
    def __init__(self, ref, copies=()):
        self.ref, self.copies, self.sent = ref, list(copies), set()

    def send(self, part=None):
        for k in range(len(self.copies)) if part is None else (part,):
            if k not in self.sent:
                self.copies[k].start()
                self.sent.add(k)

    def finish(self):
        self.send()
        for copy in self.copies:
            copy.wait()


SMALL = 80 * 1024


def run(kernel, scalars, arrays, outs, scratch=(), mib=60, parts=(), raw=()):
    parts, count = dict(parts), len(arrays)
    vmem, hbm = pl.BlockSpec(memory_space=pltpu.VMEM), pl.BlockSpec(memory_space=pltpu.HBM)
    every = [*arrays, *outs]
    large = [x.size * x.dtype.itemsize > SMALL for x in every]
    staged = [n for n in range(len(every)) if large[n] and n not in raw]
    buffers = [pltpu.VMEM(every[n].shape, every[n].dtype) for n in staged]
    semaphores = [pltpu.SemaphoreType.DMA((parts.get(n, 1),)) for n in staged]

    def body(*refs):
        lead, rest = refs[: len(scalars)], refs[len(scalars) :]
        places, rest = rest[: len(every)], rest[len(every) :]
        own, rest = rest[: len(scratch)], rest[len(scratch) :]
        boxes = []
        for n, place in enumerate(places):
            if n in raw:
                boxes.append(place)
                continue
            kind = Coming if n < count else Going
            if not large[n]:
                boxes.append(kind(place))
                continue
            at = staged.index(n)
            buffer, arrive, cuts = rest[at], rest[len(staged) + at], parts.get(n, 1)
            size = every[n].shape[0] // cuts
            copies = []
            for k in range(cuts):
                ends = [place.at[pl.ds(k * size, size)], buffer.at[pl.ds(k * size, size)]]
                source, target = ends if n < count else ends[::-1]
                copies.append(pltpu.make_async_copy(source, target, arrive.at[k]))
            boxes.append(kind(buffer, copies))
        kernel(*lead, *boxes, *own)
        for n, box in enumerate(boxes):
            if n not in raw:
                box.get() if n < count else box.finish()

    return pl.pallas_call(
        body,
        out_shape=tuple(outs),
        in_specs=[pl.BlockSpec(memory_space=pltpu.SMEM)] * len(scalars)
        + [hbm if large[n] else vmem for n in range(count)],
        out_specs=tuple(hbm if large[n] else vmem for n in range(count, len(every))),
        scratch_shapes=[*scratch, *buffers, *semaphores],
        compiler_params=pltpu.CompilerParams(vmem_limit_bytes=mib * 1024 * 1024),
        cost_estimate=pl.CostEstimate(flops=1024, bytes_accessed=1024, transcendentals=0),
    )(*scalars, *arrays)


def everyone(row):
    return lax.all_to_all(row, BOTH, 0, 0, tiled=True)


def after(value, *others):
    return lax.optimization_barrier((value, *others))[0]


def neighbours(axis):
    forward = [(i, i + 1) for i in range(lax.axis_size(axis) - 1)]
    return forward, [(j, i) for i, j in forward]


def edge_rows(blocks):
    down, up = neighbours("rows")
    last = jnp.concatenate([block[:, ROWS - 1] for block in blocks], axis=0)
    leading = jnp.concatenate([block[:, 0] for block in blocks], axis=0)
    above, below = lax.ppermute(last, "rows", down), lax.ppermute(leading, "rows", up)
    return [(above[k : k + FR], below[k : k + FR]) for k in range(0, FR * len(blocks), FR)]


def join_edges(block, edges):
    return jnp.concatenate([edges[0][:, None], block, edges[1][:, None]], axis=1)


def frame_halo(block, edges, perm):
    return lax.ppermute(join_edges(block, edges), "tm", perm).reshape(-1, C)


def flat(edges):
    return [edge.reshape(-1, C) for edge in edges]


def cells(array):
    return array.reshape(FR, ROWS, COLS, C)


def pair_sum(kept, given):
    taken = lax.ppermute(given, BOTH, CORE_PAIRS)
    return (kept.astype(F32) + taken.astype(F32)).astype(BF16)


def over_chips(pieces):
    return lax.all_to_all(pieces, BOTH, 0, 0, axis_index_groups=CHIP_GROUPS, tiled=True)


def own_share(weight):
    place = lax.axis_index(BOTH) * (SHARE // 2)
    return lax.dynamic_slice_in_dim(weight, place, SHARE // 2, axis=0).reshape(SHARE, 128)


def local(
    inputs,
    cotangent,
    gain_one,
    gain_two,
    weight_one,
    weight_two,
    first_one,
    second_one,
    first_two,
    second_two,
):
    shape = jax.ShapeDtypeStruct
    step, band = lax.axis_index("tm"), lax.axis_index("rows")
    core = (step % 2).astype(jnp.int32).reshape(1)
    inside = lambda *tests: jnp.stack([jnp.where(t, 1.0, 0.0).astype(F32) for t in tests])
    above_ok, below_ok = band > 0, band < lax.axis_size("rows") - 1
    ok_before = inside(step > 0, above_ok, below_ok)
    ok_after = inside(step < lax.axis_size("tm") - 1, above_ok, below_ok)
    gain_one, gain_two = gain_one.reshape(1, C), gain_two.reshape(1, C)
    flat_inputs, flat_cot = inputs.reshape(CELLS, C), cotangent.reshape(CELLS, C)

    row_type = shape((128, 128), F32)
    act_type, wide_type = shape((CELLS, C), BF16), shape((CELLS, C), F32)
    patch_type = shape((EXT, 3 * C), BF16)
    piece_type = shape((64, PIECE, 128), BF16)
    moment_type = shape((SHARE, 128), F32)
    patch_scratch = pltpu.VMEM((EXT, 3 * C), BF16)
    whole_scratch = pltpu.VMEM((27 * C, C), F32)
    flat_scratch = pltpu.VMEM((BLOCK + 8, 128), F32)

    def update(kernel, arrived, weight, first, second, more, part_types):
        first_new, second_new, *part = run(
            kernel,
            (),
            (*arrived, own_share(weight), first.reshape(SHARE, 128), second.reshape(SHARE, 128), *more),
            (moment_type, moment_type, *part_types),
            parts={0: 4, 6: 4} if part_types[0] is piece_type else {0: 4},
        )
        return part, first_new.reshape(-1), second_new.reshape(-1)

    forward, backward = neighbours("tm")
    edges_in, edges_cot = edge_rows((inputs, cotangent))
    (row_one,) = run(stats_kernel, (), (flat_inputs,), (row_type,))
    frames_in = frame_halo(after(inputs, row_one), edges_in, forward)
    frames_cot = frame_halo(after(cotangent, row_one), edges_cot, backward)
    table_one = everyone(row_one)
    patch_one, middle, row_two = run(
        conv_kernel,
        (ok_before,),
        (flat_inputs, *flat(edges_in), frames_in, table_one, gain_one, weight_one),
        (patch_type, act_type, row_type),
    )
    table_two = everyone(row_two)
    slope_two, row_three, kept_two, given_two = run(
        second_kernel,
        (ok_after, core),
        (flat_cot, *flat(edges_cot), frames_cot, weight_two, middle, table_two, gain_two),
        (wide_type, row_type, piece_type, piece_type),
        (patch_scratch, pltpu.VMEM((CELLS, C), F32), pltpu.VMEM((CELLS, C), BF16), whole_scratch, flat_scratch),
    )
    table_three = everyone(row_three)
    pair_two = pair_sum(kept_two, given_two)
    mid_grad, kept_one, given_one = run(
        grad_one_kernel,
        (core,),
        (after(slope_two, pair_two), middle, patch_one, table_two, table_three),
        (act_type, piece_type, piece_type),
        (whole_scratch, flat_scratch),
        parts={2: 4},
    )
    edges_grad = edge_rows((cells(mid_grad),))[0]
    frames_grad = frame_halo(cells(mid_grad), edges_grad, backward)
    arrived_two = over_chips(pair_two)
    part_two, new_first_two, new_second_two = update(
        adam_two_kernel,
        (after(arrived_two, given_one),),
        weight_two,
        first_two,
        second_two,
        (),
        (shape((1, PIECE, 128), BF16),),
    )
    gathered_two = lax.all_gather(part_two[0], BOTH, axis=0, tiled=True)
    pair_one = pair_sum(kept_one, after(given_one, part_two[0]))
    arrived_one = over_chips(pair_one)
    (part_one,), new_first_one, new_second_one = update(
        adam_one_kernel,
        (after(arrived_one, frames_grad),),
        weight_one,
        first_one,
        second_one,
        (),
        (piece_type,),
    )
    slope_one, row_four = run(
        back_one_kernel,
        (ok_after,),
        (
            after(mid_grad, part_one),
            *flat(edges_grad),
            frames_grad,
            weight_one,
            flat_inputs,
            table_one,
            gain_one,
        ),
        (wide_type, row_type),
        (patch_scratch, pltpu.VMEM((CELLS, C), F32)),
    )
    own_one = over_chips(part_one)
    other_one = lax.ppermute(after(own_one, row_four), BOTH, CORE_PAIRS)
    table_four = everyone(after(row_four, own_one))
    (input_grad,) = run(
        final_kernel, (), (slope_one, flat_inputs, table_one, table_four, flat_cot), (act_type,)
    )
    weight_type = shape((27 * C, C), BF16)
    assemble_scratch = pltpu.VMEM((2 * BLOCK + 8, 128), F32)
    (new_weight_one,) = run(
        assemble_kernel,
        (core,),
        (own_one, other_one),
        (weight_type,),
        (assemble_scratch, pltpu.VMEM((2, 64, PIECE, 128), BF16), pltpu.SemaphoreType.DMA((2, 4))),
        parts={2: 4},
        raw=(0, 1),
    )
    (new_weight_two,) = run(
        assemble_all_kernel, (), (gathered_two,), (weight_type,), (assemble_scratch,), parts={0: 4, 1: 4}
    )
    return (
        cells(input_grad),
        new_weight_one,
        new_weight_two,
        new_first_one,
        new_second_one,
        new_first_two,
        new_second_two,
    )


def solution(mesh):
    split, share = P("tm", "rows", None, None), P(("tm", "rows"))
    return jax.shard_map(
        local,
        mesh=mesh,
        in_specs=(split, split, P(), P(), P(), P(), share, share, share, share),
        out_specs=(split, P(), P(), share, share, share, share),
        check_vma=False,
    )
```

```python
import jax
import jax.numpy as jnp
from jax import lax
from jax.experimental import pallas as pl
from jax.experimental.pallas import tpu as pltpu
from jax.sharding import PartitionSpec as P

C = 256
COLS = 80
ROWS = 8
FR = 2
CELLS = FR * ROWS * COLS
EXT = (FR + 2) * (ROWS + 2) * COLS
BAND = ROWS * COLS
norm_eps = 1e-05
F32 = jnp.float32
BF16 = jnp.bfloat16
HERE = float(CELLS * 8)
TOTAL = HERE * 128.0
SCALE = (27.0 * C) ** (-0.5)
SHARE = 108
PIECE = 112
BLOCK = 432
BOTH = ("tm", "rows")
CORE_PAIRS = [(i, i ^ 4) for i in range(128)]
CHIP_GROUPS = [
    [((z * 4 + y) * 2 + core) * 4 + x for z in range(4) for y in range(4) for x in range(4)]
    for core in range(2)
]
learn_rate = 0.25
beta_one = 0.9
beta_two = 0.95
decay_rate = 0.1
adam_eps = 1e-08
first_fix = 1.0 - 0.9**10
second_fix = 1.0 - 0.95**10


def mixed(value, matrix):
    return jnp.dot(value, matrix, precision=lax.Precision.HIGHEST, preferred_element_type=F32)


def iotas(shape):
    return lax.broadcasted_iota(jnp.int32, shape, 0), lax.broadcasted_iota(jnp.int32, shape, 1)


def spread_matrix(offset):
    lane, channel = iotas((128, C))
    return jnp.where(lane == (channel >> 3) + offset, 1.0, 0.0).astype(F32)


def pack_row(first, second):
    channel, lane = iotas((C, 128))
    head = jnp.where((channel >> 3) == lane, 1.0, 0.0).astype(F32)
    tail = jnp.where((channel >> 3) + 32 == lane, 1.0, 0.0).astype(F32)
    wide = jnp.broadcast_to(first, (8, C)), jnp.broadcast_to(second, (8, C))
    row = mixed(wide[0], head) + mixed(wide[1], tail)
    return jnp.broadcast_to(row[0:1], (128, 128))


def read_norm(table):
    total = jnp.sum(table, axis=0, keepdims=True)
    center = total / 128.0
    offset = table - center
    square = jnp.sum(offset * offset, axis=0, keepdims=True)
    low, high = spread_matrix(0), spread_matrix(32)
    wide = lambda v, m: mixed(jnp.broadcast_to(v, (8, 128)), m)[0:1]
    spread = wide(total, high) + HERE * wide(square, low)
    return wide(center, low), lax.rsqrt(spread / TOTAL + norm_eps)


def read_sums(table):
    total = jnp.sum(table, axis=0, keepdims=True) / TOTAL
    wide = lambda m: mixed(jnp.broadcast_to(total, (8, 128)), m)[0:1]
    return wide(spread_matrix(0)), wide(spread_matrix(32))


def folded(values):
    return jnp.sum(values.reshape(-1, 8, C), axis=0)


def chunk(index, size=COLS):
    return pl.ds(pl.multiple_of(index * size, size), size)


def local_moments(read, count):
    zero = jnp.zeros((8, C), F32)
    sums = lax.fori_loop(0, count, lambda i, s: s + folded(read(i)), zero)
    ch_sum = jnp.sum(sums, axis=0, keepdims=True)
    r, c = iotas((C, C))
    same = jnp.where((r >> 3) == (c >> 3), 1.0, 0.0).astype(F32)
    mean = mixed(jnp.broadcast_to(ch_sum, (8, C)), same)[0:1] / HERE

    def squares(i, s):
        off = read(i) - mean
        return s + folded(off * off)

    ch_sq = jnp.sum(lax.fori_loop(0, count, squares, zero), axis=0, keepdims=True)
    return pack_row(mean / 8.0, ch_sq)


def store_shifted(target, rows, value, backward):
    col = lax.broadcasted_iota(jnp.int32, value.shape, 0)
    left = jnp.where(col == 0, 0.0, pltpu.roll(value, 1, 0))
    right = jnp.where(col == COLS - 1, 0.0, pltpu.roll(value, COLS - 1, 0))
    one, three = (right, left) if backward else (left, right)
    target[rows, 0:C] = one.astype(BF16)
    target[rows, C : 2 * C] = value.astype(BF16)
    target[rows, 2 * C : 3 * C] = three.astype(BF16)


def each_row(own, above, below, frames, ok, upcoming, target, make, backward):
    own_at, halo_at = (0, FR) if upcoming else (FR, 0)

    def put(source, i, frame, row, flag):
        value = make(source[chunk(i), :].astype(F32))
        if flag is not None:
            value = value * flag
        store_shifted(target, chunk(frame * (ROWS + 2) + row), value, backward)

    def inner(i, _):
        put(own, i, own_at + i // ROWS, i % ROWS + 1, None)
        return 0

    def edge(i, _):
        put(above, i, own_at + i, 0, ok[1])
        put(below, i, own_at + i, ROWS + 1, ok[2])
        return 0

    def outer(i, _):
        row = i % (ROWS + 2)
        flag = ok[0] * jnp.where(row == 0, ok[1], jnp.where(row == ROWS + 1, ok[2], 1.0))
        put(frames[0], i, halo_at + i // (ROWS + 2), row, flag)
        return 0

    def outer_inner(i, _):
        put(frames[0], i, halo_at + i // ROWS, i % ROWS + 1, ok[0])
        return 0

    def outer_edge(i, _):
        put(frames[1], i, halo_at + i, 0, ok[0] * ok[1])
        put(frames[2], i, halo_at + i, ROWS + 1, ok[0] * ok[2])
        return 0

    lax.fori_loop(0, FR * ROWS, inner, 0)
    lax.fori_loop(0, FR, edge, 0)
    if len(frames) == 1:
        lax.fori_loop(0, FR * (ROWS + 2), outer, 0)
    else:
        lax.fori_loop(0, FR * ROWS, outer_inner, 0)
        lax.fori_loop(0, FR, outer_edge, 0)


def conv(patches, weight, write, backward):
    for t in range(FR):
        total = None
        for a in range(3):
            for b in range(3):
                f, r = (t + 2 - a, 2 - b) if backward else (t + a, b)
                at = (f * (ROWS + 2) + r) * COLS
                left = patches[at : at + BAND, :]
                tap = (9 * a + 3 * b) * C
                if backward:
                    right = jnp.concatenate([weight[tap + k * C : tap + (k + 1) * C, :] for k in range(3)], axis=1)
                    part = lax.dot_general(left, right, (((1,), (1,)), ((), ())), preferred_element_type=F32)
                else:
                    part = jnp.dot(left, weight[tap : tap + 3 * C, :], preferred_element_type=F32)
                total = part if total is None else total + part
        write(t, total * SCALE)


def both_frames(patches, place):
    starts = [(f * (ROWS + 2) + r) * COLS for f, r in map(place, range(FR))]
    return jnp.concatenate([patches[at : at + BAND, :] for at in starts], axis=0)


def wgrad(patches, grad, whole):
    for a in range(3):
        ready = patches.get(a + FR - 1)
        for b in range(3):
            left = both_frames(ready, lambda t: (t + a, b))
            total = lax.dot_general(
                left, grad[...], (((0,), (0,)), ((), ())), preferred_element_type=F32
            )
            tap = (9 * a + 3 * b) * C
            whole[tap : tap + 3 * C, :] = total * SCALE


def cut_pieces(whole, core, flat, kept, given):
    flat[...] = jnp.zeros_like(flat)
    for side, out in ((1 - core, given), (core, kept)):

        def block(i, _):
            at = pl.multiple_of(i * BLOCK + side * (BLOCK // 2), 8)
            slab = whole[pl.ds(at, BLOCK // 2), :]
            flat[pl.ds(0, BLOCK // 2, 2), :] = slab[:, :128]
            flat[pl.ds(1, BLOCK // 2, 2), :] = slab[:, 128:]
            for x in range(4):
                out.ref[i * 4 + x] = flat[x * SHARE : x * SHARE + PIECE, :].astype(BF16)
            return 0

        lax.fori_loop(0, 16, block, 0)
        out.send()


def silu_parts(value, center, inverse, gain):
    hat = (value - center) * inverse
    pre = hat * gain
    return hat, pre, jax.nn.sigmoid(pre)


def stats_kernel(inputs, row):
    inputs = inputs.get()
    row.ref[...] = local_moments(lambda i: inputs[chunk(i), :].astype(F32), FR * ROWS)


def conv_kernel(ok, inputs, above, below, frames, table, gain, weight, patches, middle, row):
    center, inverse = read_norm(table.get()[...])
    gain = gain.get()[...]

    def hidden(value):
        _, pre, gate = silu_parts(value, center, inverse, gain)
        return pre * gate

    each_row(inputs.get(), above.get(), below.get(), (frames.get(),), ok, False, patches.ref, hidden, False)
    patches.send()

    def write(t, value):
        middle.ref[t * BAND : (t + 1) * BAND, :] = value.astype(BF16)

    conv(patches.ref, weight.get(), write, False)
    middle.send()
    row.ref[...] = local_moments(lambda i: middle.ref[chunk(i), :].astype(F32), FR * ROWS)


def slopes(read, back, center, inverse, gain, slope, hidden=None):
    def step(i, sums):
        hat, pre, gate = silu_parts(read(i), center, inverse, gain)
        if hidden is not None:
            hidden[chunk(i), :] = (pre * gate).astype(BF16)
        here = back[chunk(i), :] * gate * (1.0 + pre * (1.0 - gate)) * gain
        slope[chunk(i), :] = here
        return sums[0] + folded(here), sums[1] + folded(here * hat)

    zero = jnp.zeros((8, C), F32)
    plain, cross = lax.fori_loop(0, FR * ROWS, step, (zero, zero))
    return pack_row(jnp.sum(plain, axis=0, keepdims=True), jnp.sum(cross, axis=0, keepdims=True))


def back_two_kernel(ok, cotangent, above, below, frames, weight, back, patches):
    each_row(
        cotangent.get(), above.get(), below.get(), (frames.get(),), ok, True, patches.ref, lambda v: v, True
    )
    patches.send()

    def write(t, value):
        back.ref[t * BAND : (t + 1) * BAND, :] = value

    conv(patches.ref, weight.get(), write, True)


def second_kernel(core, middle, back, patches, table, gain, slope, row, kept, given, hidden, whole, flat):
    center, inverse = read_norm(table.get()[...])
    middle = middle.get()
    read = lambda i: middle[chunk(i), :].astype(F32)
    row.ref[...] = slopes(read, back.get(), center, inverse, gain.get()[...], slope.ref, hidden)
    slope.send()
    turned = hidden[...].astype(F32).T.astype(BF16)
    for a in (2, 1, 0):
        ready = patches.get(FR + 1 - a)
        for b in range(3):
            right = both_frames(ready, lambda t: (t + 2 - a, 2 - b))
            total = jnp.dot(turned, right, preferred_element_type=F32)
            total = total * SCALE
            for c in range(3):
                tap = (9 * a + 3 * b + c) * C
                whole[tap : tap + C, :] = total[:, c * C : (c + 1) * C]
    cut_pieces(whole, core[0], flat, kept, given)


def grad_one_kernel(core, slope, middle, patches, table, sums, mid_grad, kept, given, whole, flat):
    center, inverse = read_norm(table.get()[...])
    mean, cross = read_sums(sums.get()[...])
    slope, middle = slope.get(), middle.get()

    def step(i, _):
        hat = (middle[chunk(i), :].astype(F32) - center) * inverse
        mid_grad.ref[chunk(i), :] = (inverse * (slope[chunk(i), :] - mean - hat * cross)).astype(BF16)
        return 0

    lax.fori_loop(0, FR * ROWS, step, 0)
    mid_grad.send()
    wgrad(patches, mid_grad.ref, whole)
    cut_pieces(whole, core[0], flat, kept, given)


def back_one_kernel(
    ok, mid_grad, above, below, frames, above_frames, below_frames, weight, inputs, table, gain, slope, row, patches, back
):
    beyond = (frames.get(), above_frames.get(), below_frames.get())
    each_row(mid_grad.get(), above.get(), below.get(), beyond, ok, True, patches, lambda v: v, True)

    def write(t, value):
        back[t * BAND : (t + 1) * BAND, :] = value

    conv(patches, weight.get(), write, True)
    center, inverse = read_norm(table.get()[...])
    inputs = inputs.get()
    read = lambda i: inputs[chunk(i), :].astype(F32)
    row.ref[...] = slopes(read, back, center, inverse, gain.get()[...], slope.ref)[: row.ref.shape[0]]


def last_kernel(core, own, other, slope, inputs, table, cotangent, weight, result, flat, halves, arrive):
    copies = []
    for n, (source, place) in enumerate(((own, core[0]), (other, 1 - core[0]))):
        copies.append(pltpu.make_async_copy(source, halves.at[place], arrive.at[n]))
        copies[-1].start()
    center, inverse = read_norm(table.get()[...])
    for copy in copies:
        copy.wait()

    def block(i, _):
        assemble(i, lambda s: halves[s // 4, i * 4 + s % 4], weight.ref, flat)
        return 0

    for k in range(4):
        lax.fori_loop(4 * k, 4 * k + 4, block, 0)
        weight.send(k)

    add = lambda i, s: s + halves[0, i, 96:, :].astype(F32) + halves[1, i, 96:, :].astype(F32)
    sums = lax.fori_loop(0, 64, add, jnp.zeros((16, 128), F32))
    mean, cross = read_sums(sums[SHARE - 96 :])
    slope, inputs, cotangent = slope.get(), inputs.get(), cotangent.get()

    def step(i, _):
        hat = (inputs[chunk(i), :].astype(F32) - center) * inverse
        grad = inverse * (slope[chunk(i), :] - mean - hat * cross)
        result.ref[chunk(i), :] = (cotangent[chunk(i), :].astype(F32) + grad).astype(BF16)
        return 0

    lax.fori_loop(0, FR * ROWS, step, 0)


def adam_step(arrived, own, first, second, first_new, second_new, extra):
    gradient = jnp.zeros((PIECE, 128), F32)
    for k in range(4):
        ready = arrived.get(k)
        gradient = lax.fori_loop(16 * k, 16 * k + 16, lambda i, s: s + ready[i].astype(F32), gradient)
    gradient = gradient[:SHARE]
    one = beta_one * first.get()[...] + (1.0 - beta_one) * gradient
    two = beta_two * second.get()[...] + (1.0 - beta_two) * gradient * gradient
    first_new.ref[...] = one
    second_new.ref[...] = two
    updated = own.get()[...].astype(F32) * (1.0 - learn_rate * decay_rate) - learn_rate * (one / first_fix) / (
        jnp.sqrt(two / second_fix) + adam_eps
    )
    return jnp.concatenate([updated, extra], axis=0).astype(BF16)


def adam_two_kernel(arrived, own, first, second, first_new, second_new, part):
    extra = jnp.zeros((PIECE - SHARE, 128), F32)
    part.ref[0] = adam_step(arrived, own, first, second, first_new, second_new, extra)


def adam_one_kernel(arrived, own, first, second, sums, first_new, second_new, spread):
    rest = sums.get()[0:1, :]
    terms = []
    for _ in range(3):
        terms.append(rest.astype(BF16).astype(F32))
        rest = rest - terms[-1]
    extra = jnp.concatenate([*terms, jnp.zeros((1, 128), F32)], axis=0)
    piece = adam_step(arrived, own, first, second, first_new, second_new, extra)

    def copy(i, _):
        spread.ref[i] = piece
        return 0

    for k in range(4):
        lax.fori_loop(16 * k, 16 * k + 16, copy, 0)
        spread.send(k)


def assemble(block, piece, weight, flat):
    for s in range(8):
        flat[s * SHARE : s * SHARE + PIECE, :] = piece(s).astype(F32)
    rows = pl.ds(pl.multiple_of(block * BLOCK, BLOCK), BLOCK)
    weight[rows, 0:128] = flat[pl.ds(0, BLOCK, 2), :].astype(BF16)
    weight[rows, 128:256] = flat[pl.ds(1, BLOCK, 2), :].astype(BF16)


def assemble_all_kernel(gathered, weight, flat):
    for k in range(4):
        ready = gathered.get(k)

        def block(i, _):
            assemble(i, lambda s: ready[i * 8 + s], weight.ref, flat)
            return 0

        lax.fori_loop(4 * k, 4 * k + 4, block, 0)
        weight.send(k)


class Coming:
    def __init__(self, ref, copies=()):
        self.ref, self.copies = ref, list(copies)
        for copy in self.copies:
            copy.start()
        self.parts = len(self.copies)

    def get(self, part=None):
        last = self.parts - 1 if part is None else part
        while self.copies and self.parts - len(self.copies) <= last:
            self.copies.pop(0).wait()
        return self.ref


class Going:
    def __init__(self, ref, copies=()):
        self.ref, self.copies, self.sent = ref, list(copies), set()

    def send(self, part=None):
        for k in range(len(self.copies)) if part is None else (part,):
            if k not in self.sent:
                self.copies[k].start()
                self.sent.add(k)

    def finish(self):
        self.send()
        for copy in self.copies:
            copy.wait()


SMALL = 80 * 1024


def run(kernel, scalars, arrays, outs, scratch=(), mib=60, parts=(), raw=()):
    parts, count = dict(parts), len(arrays)
    vmem, hbm = pl.BlockSpec(memory_space=pltpu.VMEM), pl.BlockSpec(memory_space=pltpu.HBM)
    every = [*arrays, *outs]
    large = [x.size * x.dtype.itemsize > SMALL for x in every]
    staged = [n for n in range(len(every)) if large[n] and n not in raw]
    buffers = [pltpu.VMEM(every[n].shape, every[n].dtype) for n in staged]
    semaphores = [pltpu.SemaphoreType.DMA((parts.get(n, 1),)) for n in staged]

    def body(*refs):
        lead, rest = refs[: len(scalars)], refs[len(scalars) :]
        places, rest = rest[: len(every)], rest[len(every) :]
        own, rest = rest[: len(scratch)], rest[len(scratch) :]
        boxes = []
        for n, place in enumerate(places):
            if n in raw:
                boxes.append(place)
                continue
            kind = Coming if n < count else Going
            if not large[n]:
                boxes.append(kind(place))
                continue
            at = staged.index(n)
            buffer, arrive, cuts = rest[at], rest[len(staged) + at], parts.get(n, 1)
            size = every[n].shape[0] // cuts
            copies = []
            for k in range(cuts):
                ends = [place.at[pl.ds(k * size, size)], buffer.at[pl.ds(k * size, size)]]
                source, target = ends if n < count else ends[::-1]
                copies.append(pltpu.make_async_copy(source, target, arrive.at[k]))
            boxes.append(kind(buffer, copies))
        kernel(*lead, *boxes, *own)
        for n, box in enumerate(boxes):
            if n not in raw:
                box.get() if n < count else box.finish()

    return pl.pallas_call(
        body,
        out_shape=tuple(jax.ShapeDtypeStruct(x.shape, x.dtype) for x in outs),
        in_specs=[pl.BlockSpec(memory_space=pltpu.SMEM)] * len(scalars)
        + [hbm if large[n] else vmem for n in range(count)],
        out_specs=tuple(hbm if large[n] else vmem for n in range(count, len(every))),
        scratch_shapes=[*scratch, *buffers, *semaphores],
        compiler_params=pltpu.CompilerParams(vmem_limit_bytes=mib * 1024 * 1024),
        cost_estimate=pl.CostEstimate(flops=1024, bytes_accessed=1024, transcendentals=0),
    )(*scalars, *arrays)


def everyone(row):
    return lax.all_to_all(row, BOTH, 0, 0, tiled=True)


def after(value, *others):
    return lax.optimization_barrier((value, *others))[0]


def neighbours(axis):
    forward = [(i, i + 1) for i in range(lax.axis_size(axis) - 1)]
    return forward, [(j, i) for i, j in forward]


def edge_rows(last, leading, blocks):
    down, up = neighbours("rows")
    above, below = lax.ppermute(last, "rows", down), lax.ppermute(leading, "rows", up)
    return [(above[k : k + FR], below[k : k + FR]) for k in range(0, FR * blocks, FR)]


def five_sides(block):
    bands, steps = lax.axis_size("rows"), lax.axis_size("tm")
    last, leading = block[:, ROWS - 1], block[:, 0]
    _, backward = neighbours("tm")
    frames = lax.ppermute(block, "tm", backward)
    place = lambda t, r: t * bands + r
    falls = [(place(t, r), place(t - 1, r + 1)) for t in range(1, steps) for r in range(bands - 1)]
    rises = [(place(t, r), place(t - 1, r - 1)) for t in range(1, steps) for r in range(1, bands)]
    corners = lax.ppermute(last, BOTH, falls), lax.ppermute(leading, BOTH, rises)
    return ((frames, *corners), *edge_rows(last, leading, 1)[0])


def join_edges(block, edges):
    return jnp.concatenate([edges[0][:, None], block, edges[1][:, None]], axis=1)


def frame_halo(block, edges, perm):
    return lax.ppermute(join_edges(block, edges), "tm", perm).reshape(-1, C)


def flat(edges):
    return [edge.reshape(-1, C) for edge in edges]


def over_bands(piece):
    bands, here = lax.axis_size("rows"), lax.axis_index("rows")
    turned = [piece]
    for k in range(1, bands):
        turned.append(lax.ppermute(piece, "rows", [(i, (i + k) % bands) for i in range(bands)]))
    ordered = []
    for band in range(bands):
        choice = turned[0]
        for k in range(1, bands):
            choice = jnp.where((here - band) % bands == k, turned[k], choice)
        ordered.append(choice)
    return jnp.concatenate(ordered, axis=0)


def cells(array):
    return array.reshape(FR, ROWS, COLS, C)


def pair_kernel(kept, taken, result):
    for k in range(4):
        first, second = kept.get(k), taken.get(k)
        for i in range(16 * k, 16 * k + 16):
            result.ref[i] = (first[i].astype(F32) + second[i].astype(F32)).astype(BF16)
        result.send(k)


def pair_sum(kept, given):
    taken = lax.ppermute(given, BOTH, CORE_PAIRS)
    (total,) = run(pair_kernel, (), (kept, taken), (kept,), parts={0: 4, 1: 4, 2: 4})
    return total


def over_chips(pieces):
    return lax.all_to_all(pieces, BOTH, 0, 0, axis_index_groups=CHIP_GROUPS, tiled=True)


def own_share(weight):
    place = lax.axis_index(BOTH) * (SHARE // 2)
    return lax.dynamic_slice_in_dim(weight, place, SHARE // 2, axis=0).reshape(SHARE, 128)


def local(
    inputs,
    cotangent,
    gain_one,
    gain_two,
    weight_one,
    weight_two,
    first_one,
    second_one,
    first_two,
    second_two,
):
    shape = jax.ShapeDtypeStruct
    step, band = lax.axis_index("tm"), lax.axis_index("rows")
    core = (step % 2).astype(jnp.int32).reshape(1)
    inside = lambda *tests: jnp.stack([jnp.where(t, 1.0, 0.0).astype(F32) for t in tests])
    above_ok, below_ok = band > 0, band < lax.axis_size("rows") - 1
    ok_before = inside(step > 0, above_ok, below_ok)
    ok_after = inside(step < lax.axis_size("tm") - 1, above_ok, below_ok)
    gain_one, gain_two = gain_one.reshape(1, C), gain_two.reshape(1, C)
    flat_inputs, flat_cot = inputs.reshape(CELLS, C), cotangent.reshape(CELLS, C)

    row_type = shape((128, 128), F32)
    act_type, wide_type = shape((CELLS, C), BF16), shape((CELLS, C), F32)
    patch_type = shape((EXT, 3 * C), BF16)
    piece_type = shape((64, PIECE, 128), BF16)
    moment_type = shape((SHARE, 128), F32)
    patch_scratch = pltpu.VMEM((EXT, 3 * C), BF16)
    whole_scratch = pltpu.VMEM((27 * C, C), F32)
    flat_scratch = pltpu.VMEM((BLOCK + 8, 128), F32)

    def update(kernel, arrived, weight, first, second, more, part_types):
        first_new, second_new, *part = run(
            kernel,
            (),
            (*arrived, own_share(weight), first.reshape(SHARE, 128), second.reshape(SHARE, 128), *more),
            (moment_type, moment_type, *part_types),
            parts={0: 4, 7: 4} if part_types[0] is piece_type else {0: 4},
        )
        return part, first_new.reshape(-1), second_new.reshape(-1)

    forward, backward = neighbours("tm")
    first_edges = [
        jnp.concatenate([block[:, at] for block in (inputs, cotangent)], axis=0) for at in (ROWS - 1, 0)
    ]
    edges_in, edges_cot = edge_rows(*first_edges, 2)
    (row_one,) = run(stats_kernel, (), (flat_inputs,), (row_type,))
    frames_in = frame_halo(after(inputs, row_one), edges_in, forward)
    frames_cot = frame_halo(after(cotangent, row_one), edges_cot, backward)
    table_one = everyone(row_one)
    patch_one, middle, row_two = run(
        conv_kernel,
        (ok_before,),
        (flat_inputs, *flat(edges_in), frames_in, table_one, gain_one, weight_one),
        (patch_type, act_type, row_type),
    )
    table_two = everyone(row_two)
    back_two, patch_cot = run(
        back_two_kernel,
        (ok_after,),
        (after(flat_cot, row_two), *flat(edges_cot), frames_cot, weight_two),
        (wide_type, patch_type),
    )
    slope_two, row_three, kept_two, given_two = run(
        second_kernel,
        (core,),
        (middle, back_two, patch_cot, table_two, gain_two),
        (wide_type, row_type, piece_type, piece_type),
        (pltpu.VMEM((CELLS, C), BF16), whole_scratch, flat_scratch),
        parts={2: 4},
    )
    table_three = everyone(row_three)
    pair_two = pair_sum(kept_two, given_two)
    mid_grad, kept_one, given_one = run(
        grad_one_kernel,
        (core,),
        (after(slope_two, pair_two), middle, patch_one, table_two, table_three),
        (act_type, piece_type, piece_type),
        (whole_scratch, flat_scratch),
        parts={2: 4},
    )
    frames_grad, *edges_grad = five_sides(cells(mid_grad))
    arrived_two = over_chips(pair_two)
    part_two, new_first_two, new_second_two = update(
        adam_two_kernel,
        (after(arrived_two, given_one),),
        weight_two,
        first_two,
        second_two,
        (),
        (shape((1, PIECE, 128), BF16),),
    )
    gathered_two = lax.all_gather(over_bands(part_two[0]), "tm", axis=0, tiled=True)
    pair_one = after(pair_sum(kept_one, after(given_one, arrived_two, *frames_grad, *edges_grad)), part_two[0])
    arrived_one = over_chips(pair_one)
    slope_one, row_four = run(
        back_one_kernel,
        (ok_after,),
        (
            after(mid_grad, pair_one),
            *flat(edges_grad),
            *flat(frames_grad),
            weight_one,
            flat_inputs,
            table_one,
            gain_one,
        ),
        (wide_type, shape((8, 128), F32)),
        (patch_scratch, pltpu.VMEM((CELLS, C), F32)),
    )
    (part_one,), new_first_one, new_second_one = update(
        adam_one_kernel,
        (arrived_one,),
        weight_one,
        first_one,
        second_one,
        (row_four,),
        (piece_type,),
    )
    own_one = over_chips(part_one)
    other_one = lax.ppermute(own_one, BOTH, CORE_PAIRS)
    weight_type = shape((27 * C, C), BF16)
    assemble_scratch = pltpu.VMEM((2 * BLOCK + 8, 128), F32)
    (new_weight_two,) = run(
        assemble_all_kernel, (), (gathered_two,), (weight_type,), (assemble_scratch,), parts={0: 4, 1: 4}
    )
    new_weight_one, input_grad = run(
        last_kernel,
        (core,),
        (own_one, other_one, slope_one, flat_inputs, table_one, flat_cot),
        (weight_type, act_type),
        (assemble_scratch, pltpu.VMEM((2, 64, PIECE, 128), BF16), pltpu.SemaphoreType.DMA((2,))),
        parts={6: 4},
        raw=(0, 1),
    )
    return (
        cells(input_grad),
        new_weight_one,
        new_weight_two,
        new_first_one,
        new_second_one,
        new_first_two,
        new_second_two,
    )


def solution(mesh):
    split, share = P("tm", "rows", None, None), P(("tm", "rows"))
    return jax.shard_map(
        local,
        mesh=mesh,
        in_specs=(split, split, P(), P(), P(), P(), share, share, share, share),
        out_specs=(split, P(), P(), share, share, share, share),
        check_vma=False,
    )
```

```python
import jax
import jax.numpy as jnp
from jax import lax
from jax.experimental import pallas as pl
from jax.experimental.pallas import tpu as pltpu
from jax.sharding import PartitionSpec as P

C = 256
COLS = 80
ROWS = 8
FR = 2
CELLS = FR * ROWS * COLS
EXT = (FR + 2) * (ROWS + 2) * COLS
BAND = ROWS * COLS
norm_eps = 1e-05
F32 = jnp.float32
BF16 = jnp.bfloat16
HERE = float(CELLS * 8)
TOTAL = HERE * 128.0
SCALE = (27.0 * C) ** (-0.5)
SHARE = 108
PIECE = 112
BLOCK = 432
BOTH = ("tm", "rows")
CORE_PAIRS = [(i, i ^ 4) for i in range(128)]
CHIP_GROUPS = [
    [((z * 4 + y) * 2 + core) * 4 + x for z in range(4) for y in range(4) for x in range(4)]
    for core in range(2)
]
PLANE_GROUPS = [
    [((z * 4 + y) * 2 + core) * 4 + x for z in range(4) for y in range(4)]
    for core in range(2)
    for x in range(4)
]
learn_rate = 0.25
beta_one = 0.9
beta_two = 0.95
decay_rate = 0.1
adam_eps = 1e-08
first_fix = 1.0 - 0.9**10
second_fix = 1.0 - 0.95**10


def mixed(values, matrix):
    terms = []
    for rest in values:
        for _ in range(3):
            terms.append(rest.astype(BF16).astype(F32))
            rest = rest - terms[-1]
    row = lax.broadcasted_iota(jnp.int32, (16, terms[0].shape[1]), 0)
    stack = jnp.zeros(row.shape, F32)
    for n, term in enumerate(terms):
        stack = jnp.where(row == n, term, stack)
    out = jnp.dot(stack.astype(BF16), matrix.astype(BF16), preferred_element_type=F32)
    return [out[3 * n : 3 * n + 1] + out[3 * n + 1 : 3 * n + 2] + out[3 * n + 2 : 3 * n + 3] for n in range(len(values))]


def iotas(shape):
    return lax.broadcasted_iota(jnp.int32, shape, 0), lax.broadcasted_iota(jnp.int32, shape, 1)


def spread_matrix(offset):
    lane, channel = iotas((128, C))
    return jnp.where(lane == (channel >> 3) + offset, 1.0, 0.0).astype(F32)


def pack_row(first, second):
    channel, lane = iotas((C, 128))
    head = jnp.where((channel >> 3) == (lane & 31), 1.0, 0.0).astype(F32)
    heads, tails = mixed((first, second), head)
    lane = lax.broadcasted_iota(jnp.int32, (1, 128), 1)
    row = jnp.where(lane < 32, heads, jnp.where(lane < 64, tails, 0.0))
    return jnp.broadcast_to(row, (128, 128))


def read_norm(table):
    total = jnp.sum(table, axis=0, keepdims=True)
    center = total / 128.0
    offset = table - center
    square = jnp.sum(offset * offset, axis=0, keepdims=True)
    both = jnp.concatenate([spread_matrix(0), spread_matrix(32)], axis=1)
    wide = mixed((center, square, total), both)
    spread = wide[2][:, C:] + HERE * wide[1][:, :C]
    return wide[0][:, :C], lax.rsqrt(spread / TOTAL + norm_eps)


def read_sums(table):
    total = jnp.sum(table, axis=0, keepdims=True) / TOTAL
    (wide,) = mixed((total,), jnp.concatenate([spread_matrix(0), spread_matrix(32)], axis=1))
    return wide[:, :C], wide[:, C:]


def folded(values):
    return jnp.sum(values.reshape(-1, 8, C), axis=0)


def chunk(index, size=COLS):
    return pl.ds(pl.multiple_of(index * size, size), size)


def local_moments(read, count):
    zero = jnp.zeros((8, C), F32)
    sums = lax.fori_loop(0, count, lambda i, s: s + folded(read(i)), zero, unroll=2)
    ch_sum = jnp.sum(sums, axis=0, keepdims=True)
    r, c = iotas((C, C))
    same = jnp.where((r >> 3) == (c >> 3), 1.0, 0.0).astype(F32)
    mean = mixed((ch_sum,), same)[0] / HERE

    def squares(i, s):
        off = read(i) - mean
        return s + folded(off * off)

    ch_sq = jnp.sum(lax.fori_loop(0, count, squares, zero, unroll=2), axis=0, keepdims=True)
    return pack_row(mean / 8.0, ch_sq)


def store_shifted(target, rows, value, backward):
    col = lax.broadcasted_iota(jnp.int32, value.shape, 0)
    left = jnp.where(col == 0, 0.0, pltpu.roll(value, 1, 0))
    right = jnp.where(col == COLS - 1, 0.0, pltpu.roll(value, COLS - 1, 0))
    one, three = (right, left) if backward else (left, right)
    target[rows, 0:C] = one.astype(BF16)
    target[rows, C : 2 * C] = value.astype(BF16)
    target[rows, 2 * C : 3 * C] = three.astype(BF16)


def each_row(own, above, below, frames, ok, upcoming, target, make, backward):
    own_at, halo_at = (0, FR) if upcoming else (FR, 0)

    def put(source, i, frame, row, flag):
        value = make(source[chunk(i), :].astype(F32))
        if flag is not None:
            value = value * flag
        store_shifted(target, chunk(frame * (ROWS + 2) + row), value, backward)

    def inner(i, _):
        put(own, i, own_at + i // ROWS, i % ROWS + 1, None)
        return 0

    def edge(i, _):
        put(above, i, own_at + i, 0, ok[1])
        put(below, i, own_at + i, ROWS + 1, ok[2])
        return 0

    def outer(i, _):
        row = i % (ROWS + 2)
        flag = ok[0] * jnp.where(row == 0, ok[1], jnp.where(row == ROWS + 1, ok[2], 1.0))
        put(frames[0], i, halo_at + i // (ROWS + 2), row, flag)
        return 0

    def outer_inner(i, _):
        put(frames[0], i, halo_at + i // ROWS, i % ROWS + 1, ok[0])
        return 0

    def outer_edge(i, _):
        put(frames[1], i, halo_at + i, 0, ok[0] * ok[1])
        put(frames[2], i, halo_at + i, ROWS + 1, ok[0] * ok[2])
        return 0

    lax.fori_loop(0, FR * ROWS, inner, 0, unroll=2)
    lax.fori_loop(0, FR, edge, 0, unroll=2)
    if len(frames) == 1:
        lax.fori_loop(0, FR * (ROWS + 2), outer, 0, unroll=2)
    else:
        lax.fori_loop(0, FR * ROWS, outer_inner, 0)
        lax.fori_loop(0, FR, outer_edge, 0)


def conv(patches, weight, write, backward):
    for t in range(FR):
        total = None
        for a in range(3):
            for b in range(3):
                f, r = (t + 2 - a, 2 - b) if backward else (t + a, b)
                at = (f * (ROWS + 2) + r) * COLS
                left = patches[at : at + BAND, :]
                tap = (9 * a + 3 * b) * C
                if backward:
                    right = jnp.concatenate([weight[tap + k * C : tap + (k + 1) * C, :] for k in range(3)], axis=1)
                    part = lax.dot_general(left, right, (((1,), (1,)), ((), ())), preferred_element_type=F32)
                else:
                    part = jnp.dot(left, weight[tap : tap + 3 * C, :], preferred_element_type=F32)
                total = part if total is None else total + part
        write(t, total * SCALE)


def both_frames(patches, place):
    starts = [(f * (ROWS + 2) + r) * COLS for f, r in map(place, range(FR))]
    return jnp.concatenate([patches[at : at + BAND, :] for at in starts], axis=0)


def wgrad(patches, grad, whole):
    for a in range(3):
        ready = patches.get(a + FR - 1)
        for b in range(3):
            left = both_frames(ready, lambda t: (t + a, b))
            total = lax.dot_general(
                left, grad[...], (((0,), (0,)), ((), ())), preferred_element_type=F32
            )
            tap = (9 * a + 3 * b) * C
            whole[tap : tap + 3 * C, :] = total * SCALE


def cut_pieces(whole, core, kept, given):
    whole[27 * C :, :] = jnp.zeros((8, C), F32)
    for side, outs in ((1 - core, given), (core, kept)):
        for k, out in enumerate(outs):

            def block(i, _):
                at = pl.multiple_of((4 * k + i) * BLOCK + side * (BLOCK // 2), 8)
                slab = whole[pl.ds(at, BLOCK // 2 + 8), :]
                for x in range(4):
                    rows = slab[x * (SHARE // 2) : x * (SHARE // 2) + PIECE // 2, :]
                    piece = jnp.concatenate([rows[:, :128], rows[:, 128:]], axis=0)
                    out.ref[i * 4 + x] = piece.astype(BF16)
                return 0

            lax.fori_loop(0, 4, block, 0)
            out.send()


def silu_parts(value, center, inverse, gain):
    hat = (value - center) * inverse
    pre = hat * gain
    return hat, pre, jax.nn.sigmoid(pre)


def stats_kernel(inputs, row):
    inputs = inputs.get()
    row.ref[...] = local_moments(lambda i: inputs[chunk(i), :].astype(F32), FR * ROWS)


def conv_kernel(ok, inputs, above, below, frames, table, gain, weight, patches, middle, row):
    center, inverse = read_norm(table.get()[...])
    gain = gain.get()[...]

    def hidden(value):
        _, pre, gate = silu_parts(value, center, inverse, gain)
        return pre * gate

    each_row(inputs.get(), above.get(), below.get(), (frames.get(),), ok, False, patches.ref, hidden, False)
    patches.send()

    def write(t, value):
        middle.ref[t * BAND : (t + 1) * BAND, :] = value.astype(BF16)

    conv(patches.ref, weight.get(), write, False)
    middle.send()
    row.ref[...] = local_moments(lambda i: middle.ref[chunk(i), :].astype(F32), FR * ROWS)


def slopes(read, back, center, inverse, gain, slope, hidden=None):
    def step(i, sums):
        hat, pre, gate = silu_parts(read(i), center, inverse, gain)
        if hidden is not None:
            hidden[chunk(i), :] = (pre * gate).astype(BF16)
        here = back[chunk(i), :] * gate * (1.0 + pre * (1.0 - gate)) * gain
        slope[chunk(i), :] = here
        return sums[0] + folded(here), sums[1] + folded(here * hat)

    zero = jnp.zeros((8, C), F32)
    plain, cross = lax.fori_loop(0, FR * ROWS, step, (zero, zero), unroll=2)
    return pack_row(jnp.sum(plain, axis=0, keepdims=True), jnp.sum(cross, axis=0, keepdims=True))


def back_two_kernel(ok, cotangent, above, below, frames, weight, back, patches):
    each_row(
        cotangent.get(), above.get(), below.get(), (frames.get(),), ok, True, patches.ref, lambda v: v, True
    )
    patches.send()

    def write(t, value):
        back.ref[t * BAND : (t + 1) * BAND, :] = value

    conv(patches.ref, weight.get(), write, True)


def second_kernel(core, middle, back, patches, table, gain, slope, row, *refs):
    kept, given, (hidden, whole) = refs[:4], refs[4:8], refs[8:]
    center, inverse = read_norm(table.get()[...])
    middle = middle.get()
    read = lambda i: middle[chunk(i), :].astype(F32)
    row.ref[...] = slopes(read, back.get(), center, inverse, gain.get()[...], slope.ref, hidden)
    slope.send()
    turned = hidden[...].astype(F32).T.astype(BF16)
    for a in (2, 1, 0):
        ready = patches.get(FR + 1 - a)
        for b in range(3):
            right = both_frames(ready, lambda t: (t + 2 - a, 2 - b))
            total = jnp.dot(turned, right, preferred_element_type=F32)
            total = total * SCALE
            for c in range(3):
                tap = (9 * a + 3 * b + c) * C
                whole[tap : tap + C, :] = total[:, c * C : (c + 1) * C]
    cut_pieces(whole, core[0], kept, given)


def grad_one_kernel(core, slope, middle, patches, table, sums, mid_grad, *refs):
    kept, given, (whole,) = refs[:4], refs[4:8], refs[8:]
    center, inverse = read_norm(table.get()[...])
    mean, cross = read_sums(sums.get()[...])
    slope, middle = slope.get(), middle.get()

    def step(i, _):
        hat = (middle[chunk(i), :].astype(F32) - center) * inverse
        mid_grad.ref[chunk(i), :] = (inverse * (slope[chunk(i), :] - mean - hat * cross)).astype(BF16)
        return 0

    lax.fori_loop(0, FR * ROWS, step, 0, unroll=2)
    mid_grad.send()
    wgrad(patches, mid_grad.ref, whole)
    cut_pieces(whole, core[0], kept, given)


def back_one_kernel(
    ok, mid_grad, above, below, frames, above_frames, below_frames, weight, inputs, table, gain, slope, row, patches, back
):
    beyond = (frames.get(), above_frames.get(), below_frames.get())
    each_row(mid_grad.get(), above.get(), below.get(), beyond, ok, True, patches, lambda v: v, True)

    def write(t, value):
        back[t * BAND : (t + 1) * BAND, :] = value

    conv(patches, weight.get(), write, True)
    center, inverse = read_norm(table.get()[...])
    inputs = inputs.get()
    read = lambda i: inputs[chunk(i), :].astype(F32)
    row.ref[...] = slopes(read, back, center, inverse, gain.get()[...], slope.ref)[: row.ref.shape[0]]


def last_kernel(core, band, *refs):
    lines, (slope, inputs, table, cotangent, weight, result, flat, halves, arrive) = refs[:8], refs[8:]
    copies = []
    for n in range(2):
        place = core[0] if n == 0 else 1 - core[0]
        for k in range(4):
            x = lax.rem(band[0] - k + 4, 4)
            copies.append(pltpu.make_async_copy(lines[4 * n + k], halves.at[place, x], arrive.at[n, k]))
            copies[-1].start()
    center, inverse = read_norm(table.get()[...])
    for copy in copies:
        copy.wait()

    def block(i, _):
        assemble(i, lambda s: halves[s // 4, s % 4, i], weight.ref, flat)
        return 0

    for k in range(4):
        lax.fori_loop(4 * k, 4 * k + 4, block, 0)
        weight.send(k)

    def add(i, sums):
        for k in range(8):
            piece = halves[k // 4, k % 4, i, 48:, :].astype(F32)
            sums = sums + piece[:8] + piece[56:]
        return sums

    sums = lax.fori_loop(0, 16, add, jnp.zeros((8, 128), F32))
    mean, cross = read_sums(sums[6:])
    slope, inputs, cotangent = slope.get(), inputs.get(), cotangent.get()

    def step(i, _):
        hat = (inputs[chunk(i), :].astype(F32) - center) * inverse
        grad = inverse * (slope[chunk(i), :] - mean - hat * cross)
        result.ref[chunk(i), :] = (cotangent[chunk(i), :].astype(F32) + grad).astype(BF16)
        return 0

    lax.fori_loop(0, FR * ROWS, step, 0, unroll=2)


def adam_step(arrived, own, first, second, first_new, second_new, extra, flat):
    gradient = jnp.zeros((PIECE, 128), F32)
    for k in range(4):
        ready = arrived.get(k)
        gradient = lax.fori_loop(16 * k, 16 * k + 16, lambda i, s: s + ready[i].astype(F32), gradient)
    flat[pl.ds(0, PIECE // 2, 2), :] = gradient[: PIECE // 2]
    flat[pl.ds(1, PIECE // 2, 2), :] = gradient[PIECE // 2 :]
    gradient = flat[:SHARE, :]
    one = beta_one * first.get()[...] + (1.0 - beta_one) * gradient
    two = beta_two * second.get()[...] + (1.0 - beta_two) * gradient * gradient
    first_new.ref[...] = one
    second_new.ref[...] = two
    updated = own.get()[...].astype(F32) * (1.0 - learn_rate * decay_rate) - learn_rate * (one / first_fix) / (
        jnp.sqrt(two / second_fix) + adam_eps
    )
    flat[...] = jnp.concatenate([updated, extra], axis=0)
    halves = [flat[pl.ds(n, PIECE // 2, 2), :] for n in range(2)]
    return jnp.concatenate(halves, axis=0).astype(BF16)


def adam_two_kernel(arrived, own, first, second, first_new, second_new, part, flat):
    extra = jnp.zeros((PIECE - SHARE, 128), F32)
    part.ref[0] = adam_step(arrived, own, first, second, first_new, second_new, extra, flat)


def adam_one_kernel(arrived, own, first, second, sums, first_new, second_new, spread, flat):
    rest = sums.get()[0:1, :]
    terms = []
    for _ in range(3):
        terms.append(rest.astype(BF16).astype(F32))
        rest = rest - terms[-1]
    extra = jnp.concatenate([*terms, jnp.zeros((1, 128), F32)], axis=0)
    piece = adam_step(arrived, own, first, second, first_new, second_new, extra, flat)

    def copy(i, _):
        spread.ref[i] = piece
        return 0

    lax.fori_loop(0, spread.ref.shape[0], copy, 0)


def assemble(block, piece, weight, wide):
    for s in range(8):
        share = piece(s).astype(F32)
        rows = slice(s * (SHARE // 2), s * (SHARE // 2) + PIECE // 2)
        wide[rows, :128] = share[: PIECE // 2]
        wide[rows, 128:] = share[PIECE // 2 :]
    rows = pl.ds(pl.multiple_of(block * BLOCK, BLOCK), BLOCK)
    weight[rows, :] = wide[:BLOCK, :].astype(BF16)


def assemble_kernel(core, own, other, weight, flat, halves, arrive):
    parts = 4
    copies = [
        [
            pltpu.make_async_copy(
                source.at[pl.ds(16 * k, 16)], halves.at[place, pl.ds(16 * k, 16)], arrive.at[n, k]
            )
            for n, (source, place) in enumerate(((own, core[0]), (other, 1 - core[0])))
        ]
        for k in range(parts)
    ]
    for pair in copies:
        for copy in pair:
            copy.start()
    for k in range(parts):
        for copy in copies[k]:
            copy.wait()

        def block(i, _):
            assemble(i, lambda s: halves[s // 4, i * 4 + s % 4], weight.ref, flat)
            return 0

        lax.fori_loop(4 * k, 4 * k + 4, block, 0)
        weight.send(k)


class Coming:
    def __init__(self, ref, copies=()):
        self.ref, self.copies = ref, list(copies)
        for copy in self.copies:
            copy.start()
        self.parts = len(self.copies)

    def get(self, part=None):
        last = self.parts - 1 if part is None else part
        while self.copies and self.parts - len(self.copies) <= last:
            self.copies.pop(0).wait()
        return self.ref


class Going:
    def __init__(self, ref, copies=()):
        self.ref, self.copies, self.sent = ref, list(copies), set()

    def send(self, part=None):
        for k in range(len(self.copies)) if part is None else (part,):
            if k not in self.sent:
                self.copies[k].start()
                self.sent.add(k)

    def finish(self):
        self.send()
        for copy in self.copies:
            copy.wait()


SMALL, SMALL_RESULT = 16 * 1024, 80 * 1024


def run(kernel, scalars, arrays, outs, scratch=(), mib=60, parts=(), raw=()):
    parts, count = dict(parts), len(arrays)
    vmem, hbm = pl.BlockSpec(memory_space=pltpu.VMEM), pl.BlockSpec(memory_space=pl.ANY)
    every = [*arrays, *outs]
    large = [x.size * x.dtype.itemsize > (SMALL if n < count else SMALL_RESULT) for n, x in enumerate(every)]
    staged = [n for n in range(len(every)) if large[n] and n not in raw]
    buffers = [pltpu.VMEM(every[n].shape, every[n].dtype) for n in staged]
    semaphores = [pltpu.SemaphoreType.DMA((parts.get(n, 1),)) for n in staged]

    def body(*refs):
        lead, rest = refs[: len(scalars)], refs[len(scalars) :]
        places, rest = rest[: len(every)], rest[len(every) :]
        own, rest = rest[: len(scratch)], rest[len(scratch) :]
        boxes = [None] * len(every)
        for n in sorted(range(len(every)), key=lambda n: every[n].size > 128 * 128):
            place, kind = places[n], Coming if n < count else Going
            if n in raw:
                boxes[n] = place
                continue
            if not large[n]:
                boxes[n] = kind(place)
                continue
            at = staged.index(n)
            buffer, arrive, cuts = rest[at], rest[len(staged) + at], parts.get(n, 1)
            size = every[n].shape[0] // cuts
            copies = []
            for k in range(cuts):
                ends = [place.at[pl.ds(k * size, size)], buffer.at[pl.ds(k * size, size)]]
                source, target = ends if n < count else ends[::-1]
                copies.append(pltpu.make_async_copy(source, target, arrive.at[k]))
            boxes[n] = kind(buffer, copies)
        kernel(*lead, *boxes, *own)
        for n, box in enumerate(boxes):
            if n not in raw:
                box.get() if n < count else box.finish()

    return pl.pallas_call(
        body,
        out_shape=tuple(jax.ShapeDtypeStruct(x.shape, x.dtype) for x in outs),
        in_specs=[pl.BlockSpec(memory_space=pltpu.SMEM)] * len(scalars)
        + [hbm if large[n] else vmem for n in range(count)],
        out_specs=tuple(hbm if large[n] else vmem for n in range(count, len(every))),
        scratch_shapes=[*scratch, *buffers, *semaphores],
        compiler_params=pltpu.CompilerParams(vmem_limit_bytes=mib * 1024 * 1024),
        cost_estimate=pl.CostEstimate(flops=1024, bytes_accessed=1024, transcendentals=0),
    )(*scalars, *arrays)


def everyone(row):
    return lax.all_to_all(row, BOTH, 0, 0, tiled=True)


def after(value, *others):
    return lax.optimization_barrier((value, *others))[0]


def neighbours(axis):
    forward = [(i, i + 1) for i in range(lax.axis_size(axis) - 1)]
    return forward, [(j, i) for i, j in forward]


def edge_rows(last, leading, blocks):
    down, up = neighbours("rows")
    above, below = lax.ppermute(last, "rows", down), lax.ppermute(leading, "rows", up)
    return [(above[k : k + FR], below[k : k + FR]) for k in range(0, FR * blocks, FR)]


def five_sides(block):
    bands, steps = lax.axis_size("rows"), lax.axis_size("tm")
    last, leading = block[:, ROWS - 1], block[:, 0]
    _, backward = neighbours("tm")
    frames = lax.ppermute(block, "tm", backward)
    place = lambda t, r: t * bands + r
    falls = [(place(t, r), place(t - 1, r + 1)) for t in range(1, steps) for r in range(bands - 1)]
    rises = [(place(t, r), place(t - 1, r - 1)) for t in range(1, steps) for r in range(1, bands)]
    corners = lax.ppermute(last, BOTH, falls), lax.ppermute(leading, BOTH, rises)
    return ((frames, *corners), *edge_rows(last, leading, 1)[0])


def join_edges(block, edges):
    return jnp.concatenate([edges[0][:, None], block, edges[1][:, None]], axis=1)


def frame_halo(block, edges, perm):
    return lax.ppermute(join_edges(block, edges), "tm", perm).reshape(-1, C)


def flat(edges):
    return [edge.reshape(-1, C) for edge in edges]


def over_plane(pieces):
    return lax.all_to_all(pieces, BOTH, 0, 0, axis_index_groups=PLANE_GROUPS, tiled=True)


def over_line(piece):
    bands = lax.axis_size("rows")
    return [
        lax.ppermute(piece, "rows", [(i, (i + k) % bands) for i in range(bands)]) for k in range(1, bands)
    ]


def over_bands(piece):
    bands, here = lax.axis_size("rows"), lax.axis_index("rows")
    turned = [piece, *over_line(piece)]
    ordered = []
    for band in range(bands):
        choice = turned[0]
        for k in range(1, bands):
            choice = jnp.where((here - band) % bands == k, turned[k], choice)
        ordered.append(choice)
    return jnp.concatenate(ordered, axis=0)


def cells(array):
    return array.reshape(FR, ROWS, COLS, C)


def pair_kernel(*refs):
    kept, taken, result = refs[:4], refs[4:8], refs[8]
    for k in range(4):
        first, second = kept[k].get(), taken[k].get()
        for i in range(16):
            result.ref[16 * k + i] = (first[i].astype(F32) + second[i].astype(F32)).astype(BF16)
        result.send(k)


def pair_sum(kept, given):
    taken = [lax.ppermute(part, BOTH, CORE_PAIRS) for part in given]
    whole = jax.ShapeDtypeStruct((64, PIECE, 128), BF16)
    (total,) = run(pair_kernel, (), (*kept, *taken), (whole,), parts={8: 4})
    return total


def over_chips(pieces):
    return lax.all_to_all(pieces, BOTH, 0, 0, axis_index_groups=CHIP_GROUPS, tiled=True)


def own_share(weight):
    place = lax.axis_index(BOTH) * (SHARE // 2)
    return lax.dynamic_slice_in_dim(weight, place, SHARE // 2, axis=0).reshape(SHARE, 128)


def local(
    inputs,
    cotangent,
    gain_one,
    gain_two,
    weight_one,
    weight_two,
    first_one,
    second_one,
    first_two,
    second_two,
):
    shape = jax.ShapeDtypeStruct
    step, band = lax.axis_index("tm"), lax.axis_index("rows")
    core = (step % 2).astype(jnp.int32).reshape(1)
    inside = lambda *tests: jnp.stack([jnp.where(t, 1.0, 0.0).astype(F32) for t in tests])
    above_ok, below_ok = band > 0, band < lax.axis_size("rows") - 1
    ok_before = inside(step > 0, above_ok, below_ok)
    ok_after = inside(step < lax.axis_size("tm") - 1, above_ok, below_ok)
    gain_one, gain_two = gain_one.reshape(1, C), gain_two.reshape(1, C)
    flat_inputs, flat_cot = inputs.reshape(CELLS, C), cotangent.reshape(CELLS, C)

    row_type = shape((128, 128), F32)
    act_type, wide_type = shape((CELLS, C), BF16), shape((CELLS, C), F32)
    patch_type = shape((EXT, 3 * C), BF16)
    piece_types = (shape((16, PIECE, 128), BF16),) * 8
    moment_type = shape((SHARE, 128), F32)
    patch_scratch = pltpu.VMEM((EXT, 3 * C), BF16)
    whole_scratch = pltpu.VMEM((27 * C + 8, C), F32)

    def update(kernel, arrived, weight, first, second, more, part_types):
        first_new, second_new, *part = run(
            kernel,
            (),
            (*arrived, own_share(weight), first.reshape(SHARE, 128), second.reshape(SHARE, 128), *more),
            (moment_type, moment_type, *part_types),
            (pltpu.VMEM((PIECE, 128), F32),),
            parts={0: 4},
        )
        return part, first_new.reshape(-1), second_new.reshape(-1)

    forward, backward = neighbours("tm")
    first_edges = [
        jnp.concatenate([block[:, at] for block in (inputs, cotangent)], axis=0) for at in (ROWS - 1, 0)
    ]
    edges_in, edges_cot = edge_rows(*first_edges, 2)
    (row_one,) = run(stats_kernel, (), (flat_inputs,), (row_type,))
    frames_in = frame_halo(after(inputs, row_one), edges_in, forward)
    frames_cot = frame_halo(after(cotangent, row_one), edges_cot, backward)
    table_one = everyone(row_one)
    patch_one, middle, row_two = run(
        conv_kernel,
        (ok_before,),
        (flat_inputs, *flat(edges_in), frames_in, table_one, gain_one, weight_one),
        (patch_type, act_type, row_type),
    )
    table_two = everyone(row_two)
    back_two, patch_cot = run(
        back_two_kernel,
        (ok_after,),
        (after(flat_cot, row_two), *flat(edges_cot), frames_cot, weight_two),
        (wide_type, patch_type),
    )
    slope_two, row_three, *cuts_two = run(
        second_kernel,
        (core,),
        (middle, back_two, patch_cot, table_two, gain_two),
        (wide_type, row_type, *piece_types),
        (pltpu.VMEM((CELLS, C), BF16), whole_scratch),
        parts={2: 4},
    )
    table_three = everyone(row_three)
    pair_two = pair_sum(cuts_two[:4], cuts_two[4:])
    mid_grad, *cuts_one = run(
        grad_one_kernel,
        (core,),
        (after(slope_two, pair_two), middle, patch_one, table_two, table_three),
        (act_type, *piece_types),
        (whole_scratch,),
        parts={2: 4},
    )
    frames_grad, *edges_grad = five_sides(cells(mid_grad))
    arrived_two = over_chips(pair_two)
    kept_first = after(cuts_one[0], *frames_grad, *edges_grad)
    pair_one = pair_sum((kept_first, *cuts_one[1:4]), cuts_one[4:])
    part_two, new_first_two, new_second_two = update(
        adam_two_kernel,
        (after(arrived_two, pair_one),),
        weight_two,
        first_two,
        second_two,
        (),
        (shape((1, PIECE, 128), BF16),),
    )
    arrived_one = over_chips(pair_one)
    line_two = over_bands(part_two[0])
    spread_two = jnp.broadcast_to(line_two.reshape(1, 4 * PIECE, 128), (16, 4 * PIECE, 128))
    slope_one, row_four = run(
        back_one_kernel,
        (ok_after,),
        (
            after(mid_grad, pair_one),
            *flat(edges_grad),
            *flat(frames_grad),
            weight_one,
            flat_inputs,
            table_one,
            gain_one,
        ),
        (wide_type, shape((8, 128), F32)),
        (patch_scratch, pltpu.VMEM((CELLS, C), F32)),
    )
    (part_one,), new_first_one, new_second_one = update(
        adam_one_kernel,
        (after(arrived_one, line_two),),
        weight_one,
        first_one,
        second_one,
        (row_four,),
        (shape((16, PIECE, 128), BF16),),
    )
    own_one = over_plane(part_one)
    lines_one = [own_one, *over_line(own_one)]
    own_two = over_plane(after(spread_two, own_one))
    own_two = after(own_two, *lines_one)
    other_two = lax.ppermute(own_two, BOTH, CORE_PAIRS).reshape(64, PIECE, 128)
    others_one = [lax.ppermute(line, BOTH, CORE_PAIRS) for line in lines_one]
    weight_type = shape((27 * C, C), BF16)
    assemble_scratch = pltpu.VMEM((BLOCK + 8, C), F32)
    (new_weight_two,) = run(
        assemble_kernel,
        (core,),
        (own_two.reshape(64, PIECE, 128), other_two),
        (weight_type,),
        (assemble_scratch, pltpu.VMEM((2, 64, PIECE, 128), BF16), pltpu.SemaphoreType.DMA((2, 4))),
        mib=16,
        parts={2: 4},
        raw=(0, 1),
    )
    new_weight_one, input_grad = run(
        last_kernel,
        (core, band.astype(jnp.int32).reshape(1)),
        (*lines_one, *others_one, after(slope_one, new_weight_two), flat_inputs, table_one, flat_cot),
        (weight_type, act_type),
        (assemble_scratch, pltpu.VMEM((2, 4, 16, PIECE, 128), BF16), pltpu.SemaphoreType.DMA((2, 4))),
        mib=24,
        parts={12: 4},
        raw=range(8),
    )
    return (
        cells(input_grad),
        new_weight_one,
        new_weight_two,
        new_first_one,
        new_second_one,
        new_first_two,
        new_second_two,
    )


def solution(mesh):
    split, share = P("tm", "rows", None, None), P(("tm", "rows"))
    return jax.shard_map(
        local,
        mesh=mesh,
        in_specs=(split, split, P(), P(), P(), P(), share, share, share, share),
        out_specs=(split, P(), P(), share, share, share, share),
        check_vma=False,
    )
```

```python
import jax
import jax.numpy as jnp
from jax import lax
from jax.experimental import pallas as pl
from jax.experimental.pallas import tpu as pltpu
from jax.sharding import PartitionSpec as P

C = 256
COLS = 80
ROWS = 8
FR = 2
CELLS = FR * ROWS * COLS
EXT = (FR + 2) * (ROWS + 2) * COLS
BAND = ROWS * COLS
norm_eps = 1e-05
F32 = jnp.float32
BF16 = jnp.bfloat16
HERE = float(CELLS * 8)
TOTAL = HERE * 128.0
SCALE = (27.0 * C) ** (-0.5)
SHARE = 108
PIECE = 112
BLOCK = 432
BOTH = ("tm", "rows")
CORE_PAIRS = [(i, i ^ 4) for i in range(128)]
CHIP_GROUPS = [
    [((z * 4 + y) * 2 + core) * 4 + x for z in range(4) for y in range(4) for x in range(4)]
    for core in range(2)
]
PLANE_GROUPS = [
    [((z * 4 + y) * 2 + core) * 4 + x for z in range(4) for y in range(4)]
    for core in range(2)
    for x in range(4)
]
learn_rate = 0.25
beta_one = 0.9
beta_two = 0.95
decay_rate = 0.1
adam_eps = 1e-08
first_fix = 1.0 - 0.9**10
second_fix = 1.0 - 0.95**10


def mixed(values, matrix):
    terms = []
    for rest in values:
        for _ in range(3):
            terms.append(rest.astype(BF16).astype(F32))
            rest = rest - terms[-1]
    row = lax.broadcasted_iota(jnp.int32, (16, terms[0].shape[1]), 0)
    stack = jnp.zeros(row.shape, F32)
    for n, term in enumerate(terms):
        stack = jnp.where(row == n, term, stack)
    out = jnp.dot(stack.astype(BF16), matrix.astype(BF16), preferred_element_type=F32)
    return [out[3 * n : 3 * n + 1] + out[3 * n + 1 : 3 * n + 2] + out[3 * n + 2 : 3 * n + 3] for n in range(len(values))]


def iotas(shape):
    return lax.broadcasted_iota(jnp.int32, shape, 0), lax.broadcasted_iota(jnp.int32, shape, 1)


def spread_matrix(offset):
    lane, channel = iotas((128, C))
    return jnp.where(lane == (channel >> 3) + offset, 1.0, 0.0).astype(F32)


def pack_row(first, second):
    channel, lane = iotas((C, 128))
    head = jnp.where((channel >> 3) == (lane & 31), 1.0, 0.0).astype(F32)
    heads, tails = mixed((first, second), head)
    lane = lax.broadcasted_iota(jnp.int32, (1, 128), 1)
    row = jnp.where(lane < 32, heads, jnp.where(lane < 64, tails, 0.0))
    return jnp.broadcast_to(row, (128, 128))


def read_norm(table):
    total = jnp.sum(table, axis=0, keepdims=True)
    center = total / 128.0
    offset = table - center
    square = jnp.sum(offset * offset, axis=0, keepdims=True)
    both = jnp.concatenate([spread_matrix(0), spread_matrix(32)], axis=1)
    wide = mixed((center, square, total), both)
    spread = wide[2][:, C:] + HERE * wide[1][:, :C]
    return wide[0][:, :C], lax.rsqrt(spread / TOTAL + norm_eps)


def read_sums(table):
    total = jnp.sum(table, axis=0, keepdims=True) / TOTAL
    (wide,) = mixed((total,), jnp.concatenate([spread_matrix(0), spread_matrix(32)], axis=1))
    return wide[:, :C], wide[:, C:]


def folded(values):
    return jnp.sum(values.reshape(-1, 8, C), axis=0)


def chunk(index, size=COLS):
    return pl.ds(pl.multiple_of(index * size, size), size)


def local_moments(read, count):
    zero = jnp.zeros((8, C), F32)
    sums = lax.fori_loop(0, count, lambda i, s: s + folded(read(i)), zero, unroll=2)
    ch_sum = jnp.sum(sums, axis=0, keepdims=True)
    r, c = iotas((C, C))
    same = jnp.where((r >> 3) == (c >> 3), 1.0, 0.0).astype(F32)
    mean = mixed((ch_sum,), same)[0] / HERE

    def squares(i, s):
        off = read(i) - mean
        return s + folded(off * off)

    ch_sq = jnp.sum(lax.fori_loop(0, count, squares, zero, unroll=2), axis=0, keepdims=True)
    return pack_row(mean / 8.0, ch_sq)


def store_shifted(target, rows, value, backward):
    col = lax.broadcasted_iota(jnp.int32, value.shape, 0)
    left = jnp.where(col == 0, 0.0, pltpu.roll(value, 1, 0))
    right = jnp.where(col == COLS - 1, 0.0, pltpu.roll(value, COLS - 1, 0))
    one, three = (right, left) if backward else (left, right)
    target[rows, 0:C] = one.astype(BF16)
    target[rows, C : 2 * C] = value.astype(BF16)
    target[rows, 2 * C : 3 * C] = three.astype(BF16)


def each_row(own, above, below, frames, ok, upcoming, target, make, backward):
    own_at, halo_at = (0, FR) if upcoming else (FR, 0)

    def put(source, i, frame, row, flag):
        value = make(source[chunk(i), :].astype(F32))
        if flag is not None:
            value = value * flag
        store_shifted(target, chunk(frame * (ROWS + 2) + row), value, backward)

    def inner(i, _):
        put(own, i, own_at + i // ROWS, i % ROWS + 1, None)
        return 0

    def edge(i, _):
        put(above, i, own_at + i, 0, ok[1])
        put(below, i, own_at + i, ROWS + 1, ok[2])
        return 0

    def outer(i, _):
        row = i % (ROWS + 2)
        flag = ok[0] * jnp.where(row == 0, ok[1], jnp.where(row == ROWS + 1, ok[2], 1.0))
        put(frames[0], i, halo_at + i // (ROWS + 2), row, flag)
        return 0

    def outer_inner(i, _):
        put(frames[0], i, halo_at + i // ROWS, i % ROWS + 1, ok[0])
        return 0

    def outer_edge(i, _):
        put(frames[1], i, halo_at + i, 0, ok[0] * ok[1])
        put(frames[2], i, halo_at + i, ROWS + 1, ok[0] * ok[2])
        return 0

    lax.fori_loop(0, FR * ROWS, inner, 0, unroll=2)
    lax.fori_loop(0, FR, edge, 0, unroll=2)
    if len(frames) == 1:
        lax.fori_loop(0, FR * (ROWS + 2), outer, 0, unroll=2)
    else:
        lax.fori_loop(0, FR * ROWS, outer_inner, 0)
        lax.fori_loop(0, FR, outer_edge, 0)


def conv(patches, weight, write, backward):
    for t in range(FR):
        total = None
        for a in range(3):
            for b in range(3):
                f, r = (t + 2 - a, 2 - b) if backward else (t + a, b)
                at = (f * (ROWS + 2) + r) * COLS
                left = patches[at : at + BAND, :]
                tap = (9 * a + 3 * b) * C
                if backward:
                    right = jnp.concatenate([weight[tap + k * C : tap + (k + 1) * C, :] for k in range(3)], axis=1)
                    part = lax.dot_general(left, right, (((1,), (1,)), ((), ())), preferred_element_type=F32)
                else:
                    part = jnp.dot(left, weight[tap : tap + 3 * C, :], preferred_element_type=F32)
                total = part if total is None else total + part
        write(t, total * SCALE)


def both_frames(patches, place):
    starts = [(f * (ROWS + 2) + r) * COLS for f, r in map(place, range(FR))]
    return jnp.concatenate([patches[at : at + BAND, :] for at in starts], axis=0)


def cut_blocks(blocks, whole, core, kept, given):
    for i in blocks:
        for side, outs in ((1 - core, given), (core, kept)):
            at = pl.multiple_of(i * BLOCK + side * (BLOCK // 2), 8)
            slab = whole[pl.ds(at, BLOCK // 2 + 8), :]
            for x in range(4):
                rows = slab[x * (SHARE // 2) : x * (SHARE // 2) + PIECE // 2, :]
                piece = jnp.concatenate([rows[:, :128], rows[:, 128:]], axis=0)
                outs[i // 4].ref[i % 4 * 4 + x] = piece.astype(BF16)
            if i % 4 == 3:
                outs[i // 4].send()


def wgrad(product, whole, core, kept, given):
    done = 0
    whole[27 * C :, :] = jnp.zeros((8, C), F32)
    for a in range(3):
        for b in range(3):
            tap = (9 * a + 3 * b) * C
            product(a, b, whole.at[tap : tap + 3 * C, :])
            ready = (tap + 3 * C) // BLOCK
            cut_blocks(range(done, ready), whole, core, kept, given)
            done = ready


def silu_parts(value, center, inverse, gain):
    hat = (value - center) * inverse
    pre = hat * gain
    return hat, pre, jax.nn.sigmoid(pre)


def stats_kernel(inputs, row):
    inputs = inputs.get()
    row.ref[...] = local_moments(lambda i: inputs[chunk(i), :].astype(F32), FR * ROWS)


def conv_kernel(ok, inputs, above, below, frames, table, gain, weight, patches, middle, row):
    center, inverse = read_norm(table.get()[...])
    gain = gain.get()[...]

    def hidden(value):
        _, pre, gate = silu_parts(value, center, inverse, gain)
        return pre * gate

    each_row(inputs.get(), above.get(), below.get(), (frames.get(),), ok, False, patches.ref, hidden, False)
    patches.send()

    def write(t, value):
        middle.ref[t * BAND : (t + 1) * BAND, :] = value.astype(BF16)

    conv(patches.ref, weight.get(), write, False)
    middle.send()
    row.ref[...] = local_moments(lambda i: middle.ref[chunk(i), :].astype(F32), FR * ROWS)


def slopes(read, back, center, inverse, gain, slope, hidden=None):
    def step(i, sums):
        hat, pre, gate = silu_parts(read(i), center, inverse, gain)
        if hidden is not None:
            hidden[chunk(i), :] = (pre * gate).astype(BF16)
        here = back[chunk(i), :] * gate * (1.0 + pre * (1.0 - gate)) * gain
        slope[chunk(i), :] = here
        return sums[0] + folded(here), sums[1] + folded(here * hat)

    zero = jnp.zeros((8, C), F32)
    plain, cross = lax.fori_loop(0, FR * ROWS, step, (zero, zero), unroll=2)
    return pack_row(jnp.sum(plain, axis=0, keepdims=True), jnp.sum(cross, axis=0, keepdims=True))


def back_two_kernel(ok, cotangent, above, below, frames, weight, back, patches):
    each_row(
        cotangent.get(), above.get(), below.get(), (frames.get(),), ok, True, patches.ref, lambda v: v, True
    )
    patches.send()

    def write(t, value):
        back.ref[t * BAND : (t + 1) * BAND, :] = value

    conv(patches.ref, weight.get(), write, True)


def second_kernel(core, middle, back, patches, table, gain, slope, row, *refs):
    kept, given, (hidden, whole) = refs[:4], refs[4:8], refs[8:]
    center, inverse = read_norm(table.get()[...])
    middle = middle.get()
    read = lambda i: middle[chunk(i), :].astype(F32)
    row.ref[...] = slopes(read, back.get(), center, inverse, gain.get()[...], slope.ref, hidden)
    slope.send()
    turned = hidden[...].astype(F32).T.astype(BF16)
    patches = patches.get()

    def product(a, b, rows):
        right = both_frames(patches, lambda t: (t + 2 - a, 2 - b))
        total = jnp.dot(turned, right, preferred_element_type=F32) * SCALE
        for c in range(3):
            rows[c * C : (c + 1) * C, :] = total[:, c * C : (c + 1) * C]

    wgrad(product, whole, core[0], kept, given)


def grad_one_kernel(core, slope, middle, patches, table, sums, mid_grad, *refs):
    kept, given, (whole,) = refs[:4], refs[4:8], refs[8:]
    center, inverse = read_norm(table.get()[...])
    mean, cross = read_sums(sums.get()[...])
    slope, middle = slope.get(), middle.get()

    def step(i, _):
        hat = (middle[chunk(i), :].astype(F32) - center) * inverse
        mid_grad.ref[chunk(i), :] = (inverse * (slope[chunk(i), :] - mean - hat * cross)).astype(BF16)
        return 0

    lax.fori_loop(0, FR * ROWS, step, 0, unroll=2)
    mid_grad.send()

    def product(a, b, rows):
        left = both_frames(patches.get(a + FR - 1), lambda t: (t + a, b))
        grad = mid_grad.ref[...]
        total = lax.dot_general(left, grad, (((0,), (0,)), ((), ())), preferred_element_type=F32)
        rows[...] = total * SCALE

    wgrad(product, whole, core[0], kept, given)


def back_one_kernel(
    ok, mid_grad, above, below, frames, above_frames, below_frames, weight, inputs, table, gain, slope, row, patches, back
):
    beyond = (frames.get(), above_frames.get(), below_frames.get())
    each_row(mid_grad.get(), above.get(), below.get(), beyond, ok, True, patches, lambda v: v, True)

    def write(t, value):
        back[t * BAND : (t + 1) * BAND, :] = value

    conv(patches, weight.get(), write, True)
    center, inverse = read_norm(table.get()[...])
    inputs = inputs.get()
    read = lambda i: inputs[chunk(i), :].astype(F32)
    row.ref[...] = slopes(read, back, center, inverse, gain.get()[...], slope.ref)[: row.ref.shape[0]]


def last_kernel(core, band, *refs):
    lines, (slope, inputs, table, cotangent, weight, result, flat, halves, arrive) = refs[:8], refs[8:]
    copies = []
    for n in range(2):
        place = core[0] if n == 0 else 1 - core[0]
        for k in range(4):
            x = lax.rem(band[0] - k + 4, 4)
            copies.append(pltpu.make_async_copy(lines[4 * n + k], halves.at[place, x], arrive.at[n, k]))
            copies[-1].start()
    center, inverse = read_norm(table.get()[...])
    for copy in copies:
        copy.wait()

    def block(i, _):
        assemble(i, lambda s: halves[s // 4, s % 4, i], weight.ref, flat)
        return 0

    for k in range(4):
        lax.fori_loop(4 * k, 4 * k + 4, block, 0)
        weight.send(k)

    def add(i, sums):
        for k in range(8):
            piece = halves[k // 4, k % 4, i, 48:, :].astype(F32)
            sums = sums + piece[:8] + piece[56:]
        return sums

    sums = lax.fori_loop(0, 16, add, jnp.zeros((8, 128), F32))
    mean, cross = read_sums(sums[6:])
    slope, inputs, cotangent = slope.get(), inputs.get(), cotangent.get()

    def step(i, _):
        hat = (inputs[chunk(i), :].astype(F32) - center) * inverse
        grad = inverse * (slope[chunk(i), :] - mean - hat * cross)
        result.ref[chunk(i), :] = (cotangent[chunk(i), :].astype(F32) + grad).astype(BF16)
        return 0

    lax.fori_loop(0, FR * ROWS, step, 0, unroll=2)


def adam_step(arrived, own, first, second, first_new, second_new, extra, flat):
    gradient = jnp.zeros((PIECE, 128), F32)
    for k in range(4):
        ready = arrived.get(k)
        gradient = lax.fori_loop(16 * k, 16 * k + 16, lambda i, s: s + ready[i].astype(F32), gradient)
    flat[pl.ds(0, PIECE // 2, 2), :] = gradient[: PIECE // 2]
    flat[pl.ds(1, PIECE // 2, 2), :] = gradient[PIECE // 2 :]
    gradient = flat[:SHARE, :]
    one = beta_one * first.get()[...] + (1.0 - beta_one) * gradient
    two = beta_two * second.get()[...] + (1.0 - beta_two) * gradient * gradient
    first_new.ref[...] = one
    second_new.ref[...] = two
    updated = own.get()[...].astype(F32) * (1.0 - learn_rate * decay_rate) - learn_rate * (one / first_fix) / (
        jnp.sqrt(two / second_fix) + adam_eps
    )
    flat[...] = jnp.concatenate([updated, extra], axis=0)
    halves = [flat[pl.ds(n, PIECE // 2, 2), :] for n in range(2)]
    return jnp.concatenate(halves, axis=0).astype(BF16)


def adam_two_kernel(arrived, own, first, second, first_new, second_new, part, flat):
    extra = jnp.zeros((PIECE - SHARE, 128), F32)
    part.ref[0] = adam_step(arrived, own, first, second, first_new, second_new, extra, flat)


def adam_one_kernel(arrived, own, first, second, sums, first_new, second_new, spread, flat):
    rest = sums.get()[0:1, :]
    terms = []
    for _ in range(3):
        terms.append(rest.astype(BF16).astype(F32))
        rest = rest - terms[-1]
    extra = jnp.concatenate([*terms, jnp.zeros((1, 128), F32)], axis=0)
    piece = adam_step(arrived, own, first, second, first_new, second_new, extra, flat)

    def copy(i, _):
        spread.ref[i] = piece
        return 0

    lax.fori_loop(0, spread.ref.shape[0], copy, 0)


def assemble(block, piece, weight, wide):
    for s in range(8):
        share = piece(s).astype(F32)
        rows = slice(s * (SHARE // 2), s * (SHARE // 2) + PIECE // 2)
        wide[rows, :128] = share[: PIECE // 2]
        wide[rows, 128:] = share[PIECE // 2 :]
    rows = pl.ds(pl.multiple_of(block * BLOCK, BLOCK), BLOCK)
    weight[rows, :] = wide[:BLOCK, :].astype(BF16)


def assemble_kernel(core, own, other, weight, flat, halves, arrive):
    parts = 4
    copies = [
        [
            pltpu.make_async_copy(
                source.at[pl.ds(16 * k, 16)], halves.at[place, pl.ds(16 * k, 16)], arrive.at[n, k]
            )
            for n, (source, place) in enumerate(((own, core[0]), (other, 1 - core[0])))
        ]
        for k in range(parts)
    ]
    for pair in copies:
        for copy in pair:
            copy.start()
    for k in range(parts):
        for copy in copies[k]:
            copy.wait()

        def block(i, _):
            assemble(i, lambda s: halves[s // 4, i * 4 + s % 4], weight.ref, flat)
            return 0

        lax.fori_loop(4 * k, 4 * k + 4, block, 0)
        weight.send(k)


class Coming:
    def __init__(self, ref, copies=()):
        self.ref, self.copies = ref, list(copies)
        for copy in self.copies:
            copy.start()
        self.parts = len(self.copies)

    def get(self, part=None):
        last = self.parts - 1 if part is None else part
        while self.copies and self.parts - len(self.copies) <= last:
            self.copies.pop(0).wait()
        return self.ref


class Going:
    def __init__(self, ref, copies=()):
        self.ref, self.copies, self.sent = ref, list(copies), set()

    def send(self, part=None):
        for k in range(len(self.copies)) if part is None else (part,):
            if k not in self.sent:
                self.copies[k].start()
                self.sent.add(k)

    def finish(self):
        self.send()
        for copy in self.copies:
            copy.wait()


SMALL, SMALL_RESULT = 16 * 1024, 80 * 1024


def run(kernel, scalars, arrays, outs, scratch=(), mib=60, parts=(), raw=()):
    parts, count = dict(parts), len(arrays)
    vmem, hbm = pl.BlockSpec(memory_space=pltpu.VMEM), pl.BlockSpec(memory_space=pl.ANY)
    every = [*arrays, *outs]
    large = [x.size * x.dtype.itemsize > (SMALL if n < count else SMALL_RESULT) for n, x in enumerate(every)]
    staged = [n for n in range(len(every)) if large[n] and n not in raw]
    buffers = [pltpu.VMEM(every[n].shape, every[n].dtype) for n in staged]
    semaphores = [pltpu.SemaphoreType.DMA((parts.get(n, 1),)) for n in staged]

    def body(*refs):
        lead, rest = refs[: len(scalars)], refs[len(scalars) :]
        places, rest = rest[: len(every)], rest[len(every) :]
        own, rest = rest[: len(scratch)], rest[len(scratch) :]
        boxes = [None] * len(every)
        for n in sorted(range(len(every)), key=lambda n: every[n].size > 128 * 128):
            place, kind = places[n], Coming if n < count else Going
            if n in raw:
                boxes[n] = place
                continue
            if not large[n]:
                boxes[n] = kind(place)
                continue
            at = staged.index(n)
            buffer, arrive, cuts = rest[at], rest[len(staged) + at], parts.get(n, 1)
            size = every[n].shape[0] // cuts
            copies = []
            for k in range(cuts):
                ends = [place.at[pl.ds(k * size, size)], buffer.at[pl.ds(k * size, size)]]
                source, target = ends if n < count else ends[::-1]
                copies.append(pltpu.make_async_copy(source, target, arrive.at[k]))
            boxes[n] = kind(buffer, copies)
        kernel(*lead, *boxes, *own)
        for n, box in enumerate(boxes):
            if n not in raw:
                box.get() if n < count else box.finish()

    return pl.pallas_call(
        body,
        out_shape=tuple(jax.ShapeDtypeStruct(x.shape, x.dtype) for x in outs),
        in_specs=[pl.BlockSpec(memory_space=pltpu.SMEM)] * len(scalars)
        + [hbm if large[n] else vmem for n in range(count)],
        out_specs=tuple(hbm if large[n] else vmem for n in range(count, len(every))),
        scratch_shapes=[*scratch, *buffers, *semaphores],
        compiler_params=pltpu.CompilerParams(vmem_limit_bytes=mib * 1024 * 1024),
        cost_estimate=pl.CostEstimate(flops=1024, bytes_accessed=1024, transcendentals=0),
    )(*scalars, *arrays)


def everyone(row):
    return lax.all_to_all(row, BOTH, 0, 0, tiled=True)


def after(value, *others):
    return lax.optimization_barrier((value, *others))[0]


def neighbours(axis):
    forward = [(i, i + 1) for i in range(lax.axis_size(axis) - 1)]
    return forward, [(j, i) for i, j in forward]


def edge_rows(last, leading, blocks):
    down, up = neighbours("rows")
    above, below = lax.ppermute(last, "rows", down), lax.ppermute(leading, "rows", up)
    return [(above[k : k + FR], below[k : k + FR]) for k in range(0, FR * blocks, FR)]


def five_sides(block):
    bands, steps = lax.axis_size("rows"), lax.axis_size("tm")
    last, leading = block[:, ROWS - 1], block[:, 0]
    _, backward = neighbours("tm")
    frames = lax.ppermute(block, "tm", backward)
    place = lambda t, r: t * bands + r
    falls = [(place(t, r), place(t - 1, r + 1)) for t in range(1, steps) for r in range(bands - 1)]
    rises = [(place(t, r), place(t - 1, r - 1)) for t in range(1, steps) for r in range(1, bands)]
    corners = lax.ppermute(last, BOTH, falls), lax.ppermute(leading, BOTH, rises)
    return ((frames, *corners), *edge_rows(last, leading, 1)[0])


def join_edges(block, edges):
    return jnp.concatenate([edges[0][:, None], block, edges[1][:, None]], axis=1)


def frame_halo(block, edges, perm):
    return lax.ppermute(join_edges(block, edges), "tm", perm).reshape(-1, C)


def flat(edges):
    return [edge.reshape(-1, C) for edge in edges]


def over_plane(pieces):
    return lax.all_to_all(pieces, BOTH, 0, 0, axis_index_groups=PLANE_GROUPS, tiled=True)


def over_line(piece):
    bands = lax.axis_size("rows")
    return [
        lax.ppermute(piece, "rows", [(i, (i + k) % bands) for i in range(bands)]) for k in range(1, bands)
    ]


def over_bands(piece):
    bands, here = lax.axis_size("rows"), lax.axis_index("rows")
    turned = [piece, *over_line(piece)]
    ordered = []
    for band in range(bands):
        choice = turned[0]
        for k in range(1, bands):
            choice = jnp.where((here - band) % bands == k, turned[k], choice)
        ordered.append(choice)
    return jnp.concatenate(ordered, axis=0)


def cells(array):
    return array.reshape(FR, ROWS, COLS, C)


def pair_kernel(*refs):
    kept, taken, result = refs[:4], refs[4:8], refs[8]
    for k in range(4):
        first, second = kept[k].get(), taken[k].get()
        for i in range(16):
            result.ref[16 * k + i] = (first[i].astype(F32) + second[i].astype(F32)).astype(BF16)
        result.send(k)


def pair_sum(kept, given):
    taken = [lax.ppermute(part, BOTH, CORE_PAIRS) for part in given]
    whole = jax.ShapeDtypeStruct((64, PIECE, 128), BF16)
    (total,) = run(pair_kernel, (), (*kept, *taken), (whole,), parts={8: 4}, mib=63)
    return total


def over_chips(pieces):
    return lax.all_to_all(pieces, BOTH, 0, 0, axis_index_groups=CHIP_GROUPS, tiled=True)


def own_share(weight):
    place = lax.axis_index(BOTH) * (SHARE // 2)
    return lax.dynamic_slice_in_dim(weight, place, SHARE // 2, axis=0).reshape(SHARE, 128)


def local(
    inputs,
    cotangent,
    gain_one,
    gain_two,
    weight_one,
    weight_two,
    first_one,
    second_one,
    first_two,
    second_two,
):
    shape = jax.ShapeDtypeStruct
    step, band = lax.axis_index("tm"), lax.axis_index("rows")
    core = (step % 2).astype(jnp.int32).reshape(1)
    inside = lambda *tests: jnp.stack([jnp.where(t, 1.0, 0.0).astype(F32) for t in tests])
    above_ok, below_ok = band > 0, band < lax.axis_size("rows") - 1
    ok_before = inside(step > 0, above_ok, below_ok)
    ok_after = inside(step < lax.axis_size("tm") - 1, above_ok, below_ok)
    gain_one, gain_two = gain_one.reshape(1, C), gain_two.reshape(1, C)
    flat_inputs, flat_cot = inputs.reshape(CELLS, C), cotangent.reshape(CELLS, C)

    row_type = shape((128, 128), F32)
    act_type, wide_type = shape((CELLS, C), BF16), shape((CELLS, C), F32)
    patch_type = shape((EXT, 3 * C), BF16)
    piece_types = (shape((16, PIECE, 128), BF16),) * 8
    moment_type = shape((SHARE, 128), F32)
    patch_scratch = pltpu.VMEM((EXT, 3 * C), BF16)
    whole_scratch = pltpu.VMEM((27 * C + 8, C), F32)

    def update(kernel, arrived, weight, first, second, more, part_types):
        first_new, second_new, *part = run(
            kernel,
            (),
            (*arrived, own_share(weight), first.reshape(SHARE, 128), second.reshape(SHARE, 128), *more),
            (moment_type, moment_type, *part_types),
            (pltpu.VMEM((PIECE, 128), F32),),
            parts={0: 4},
        )
        return part, first_new.reshape(-1), second_new.reshape(-1)

    forward, backward = neighbours("tm")
    first_edges = [
        jnp.concatenate([block[:, at] for block in (inputs, cotangent)], axis=0) for at in (ROWS - 1, 0)
    ]
    edges_in, edges_cot = edge_rows(*first_edges, 2)
    (row_one,) = run(stats_kernel, (), (flat_inputs,), (row_type,))
    frames_in = frame_halo(after(inputs, row_one), edges_in, forward)
    frames_cot = frame_halo(after(cotangent, row_one), edges_cot, backward)
    table_one = everyone(row_one)
    patch_one, middle, row_two = run(
        conv_kernel,
        (ok_before,),
        (flat_inputs, *flat(edges_in), frames_in, table_one, gain_one, weight_one),
        (patch_type, act_type, row_type),
    )
    table_two = everyone(row_two)
    back_two, patch_cot = run(
        back_two_kernel,
        (ok_after,),
        (after(flat_cot, row_two), *flat(edges_cot), frames_cot, weight_two),
        (wide_type, patch_type),
    )
    slope_two, row_three, *cuts_two = run(
        second_kernel,
        (core,),
        (middle, back_two, patch_cot, table_two, gain_two),
        (wide_type, row_type, *piece_types),
        (pltpu.VMEM((CELLS, C), BF16), whole_scratch),
        parts={2: 4},
    )
    table_three = everyone(row_three)
    pair_two = pair_sum(cuts_two[:4], cuts_two[4:])
    mid_grad, *cuts_one = run(
        grad_one_kernel,
        (core,),
        (after(slope_two, pair_two), middle, patch_one, table_two, table_three),
        (act_type, *piece_types),
        (whole_scratch,),
        parts={2: 4},
    )
    frames_grad, *edges_grad = five_sides(cells(mid_grad))
    arrived_two = over_chips(pair_two)
    kept_first = after(cuts_one[0], *frames_grad, *edges_grad)
    pair_one = pair_sum((kept_first, *cuts_one[1:4]), cuts_one[4:])
    part_two, new_first_two, new_second_two = update(
        adam_two_kernel,
        (after(arrived_two, pair_one),),
        weight_two,
        first_two,
        second_two,
        (),
        (shape((1, PIECE, 128), BF16),),
    )
    arrived_one = over_chips(pair_one)
    line_two = over_bands(part_two[0])
    spread_two = jnp.broadcast_to(line_two.reshape(1, 4 * PIECE, 128), (16, 4 * PIECE, 128))
    slope_one, row_four = run(
        back_one_kernel,
        (ok_after,),
        (
            after(mid_grad, pair_one),
            *flat(edges_grad),
            *flat(frames_grad),
            weight_one,
            flat_inputs,
            table_one,
            gain_one,
        ),
        (wide_type, shape((8, 128), F32)),
        (patch_scratch, pltpu.VMEM((CELLS, C), F32)),
    )
    (part_one,), new_first_one, new_second_one = update(
        adam_one_kernel,
        (after(arrived_one, line_two),),
        weight_one,
        first_one,
        second_one,
        (row_four,),
        (shape((16, PIECE, 128), BF16),),
    )
    own_one = over_plane(part_one)
    lines_one = [own_one, *over_line(own_one)]
    own_two = over_plane(after(spread_two, own_one))
    own_two = after(own_two, *lines_one)
    other_two = lax.ppermute(own_two, BOTH, CORE_PAIRS).reshape(64, PIECE, 128)
    others_one = [lax.ppermute(line, BOTH, CORE_PAIRS) for line in lines_one]
    weight_type = shape((27 * C, C), BF16)
    assemble_scratch = pltpu.VMEM((BLOCK + 8, C), F32)
    (new_weight_two,) = run(
        assemble_kernel,
        (core,),
        (own_two.reshape(64, PIECE, 128), other_two),
        (weight_type,),
        (assemble_scratch, pltpu.VMEM((2, 64, PIECE, 128), BF16), pltpu.SemaphoreType.DMA((2, 4))),
        mib=16,
        parts={2: 4},
        raw=(0, 1),
    )
    new_weight_one, input_grad = run(
        last_kernel,
        (core, band.astype(jnp.int32).reshape(1)),
        (*lines_one, *others_one, after(slope_one, new_weight_two), flat_inputs, table_one, flat_cot),
        (weight_type, act_type),
        (assemble_scratch, pltpu.VMEM((2, 4, 16, PIECE, 128), BF16), pltpu.SemaphoreType.DMA((2, 4))),
        mib=24,
        parts={12: 4},
        raw=range(8),
    )
    return (
        cells(input_grad),
        new_weight_one,
        new_weight_two,
        new_first_one,
        new_second_one,
        new_first_two,
        new_second_two,
    )


def solution(mesh):
    split, share = P("tm", "rows", None, None), P(("tm", "rows"))
    return jax.shard_map(
        local,
        mesh=mesh,
        in_specs=(split, split, P(), P(), P(), P(), share, share, share, share),
        out_specs=(split, P(), P(), share, share, share, share),
        check_vma=False,
    )
```

```python
import jax
import jax.numpy as jnp
from jax import lax
from jax.experimental import pallas as pl
from jax.experimental.pallas import tpu as pltpu
from jax.sharding import PartitionSpec as P

C = 256
COLS = 80
ROWS = 8
FR = 2
CELLS = FR * ROWS * COLS
EXT = (FR + 2) * (ROWS + 2) * COLS
BAND = ROWS * COLS
norm_eps = 1e-05
F32 = jnp.float32
BF16 = jnp.bfloat16
HERE = float(CELLS * 8)
TOTAL = HERE * 128.0
SCALE = (27.0 * C) ** (-0.5)
SHARE = 108
PIECE = 112
BLOCK = 432
BOTH = ("tm", "rows")
CORE_PAIRS = [(i, i ^ 4) for i in range(128)]
CHIP_GROUPS = [
    [((z * 4 + y) * 2 + core) * 4 + x for z in range(4) for y in range(4) for x in range(4)]
    for core in range(2)
]
PLANE_GROUPS = [
    [((z * 4 + y) * 2 + core) * 4 + x for z in range(4) for y in range(4)]
    for core in range(2)
    for x in range(4)
]
learn_rate = 0.25
beta_one = 0.9
beta_two = 0.95
decay_rate = 0.1
adam_eps = 1e-08
first_fix = 1.0 - 0.9**10
second_fix = 1.0 - 0.95**10


def mixed(values, matrix):
    terms = []
    for rest in values:
        for _ in range(3):
            terms.append(rest.astype(BF16).astype(F32))
            rest = rest - terms[-1]
    row = lax.broadcasted_iota(jnp.int32, (16, terms[0].shape[1]), 0)
    stack = jnp.zeros(row.shape, F32)
    for n, term in enumerate(terms):
        stack = jnp.where(row == n, term, stack)
    out = jnp.dot(stack.astype(BF16), matrix.astype(BF16), preferred_element_type=F32)
    return [out[3 * n : 3 * n + 1] + out[3 * n + 1 : 3 * n + 2] + out[3 * n + 2 : 3 * n + 3] for n in range(len(values))]


def iotas(shape):
    return lax.broadcasted_iota(jnp.int32, shape, 0), lax.broadcasted_iota(jnp.int32, shape, 1)


def spread_matrix(offset):
    lane, channel = iotas((128, C))
    return jnp.where(lane == (channel >> 3) + offset, 1.0, 0.0).astype(F32)


def pack_row(first, second):
    channel, lane = iotas((C, 128))
    head = jnp.where((channel >> 3) == (lane & 31), 1.0, 0.0).astype(F32)
    heads, tails = mixed((first, second), head)
    lane = lax.broadcasted_iota(jnp.int32, (1, 128), 1)
    row = jnp.where(lane < 32, heads, jnp.where(lane < 64, tails, 0.0))
    return jnp.broadcast_to(row, (128, 128))


def read_norm(table):
    total = jnp.sum(table, axis=0, keepdims=True)
    center = total / 128.0
    offset = table - center
    square = jnp.sum(offset * offset, axis=0, keepdims=True)
    both = jnp.concatenate([spread_matrix(0), spread_matrix(32)], axis=1)
    wide = mixed((center, square, total), both)
    spread = wide[2][:, C:] + HERE * wide[1][:, :C]
    return wide[0][:, :C], lax.rsqrt(spread / TOTAL + norm_eps)


def read_sums(table):
    total = jnp.sum(table, axis=0, keepdims=True) / TOTAL
    (wide,) = mixed((total,), jnp.concatenate([spread_matrix(0), spread_matrix(32)], axis=1))
    return wide[:, :C], wide[:, C:]


def folded(values):
    return jnp.sum(values.reshape(-1, 8, C), axis=0)


def chunk(index, size=COLS):
    return pl.ds(pl.multiple_of(index * size, size), size)


def local_moments(read, count):
    zero = jnp.zeros((8, C), F32)
    sums = lax.fori_loop(0, count, lambda i, s: s + folded(read(i)), zero, unroll=2)
    ch_sum = jnp.sum(sums, axis=0, keepdims=True)
    r, c = iotas((C, C))
    same = jnp.where((r >> 3) == (c >> 3), 1.0, 0.0).astype(F32)
    mean = mixed((ch_sum,), same)[0] / HERE

    def squares(i, s):
        off = read(i) - mean
        return s + folded(off * off)

    ch_sq = jnp.sum(lax.fori_loop(0, count, squares, zero, unroll=2), axis=0, keepdims=True)
    return pack_row(mean / 8.0, ch_sq)


def store_shifted(target, rows, value, backward):
    col = lax.broadcasted_iota(jnp.int32, value.shape, 0)
    left = jnp.where(col == 0, 0.0, pltpu.roll(value, 1, 0))
    right = jnp.where(col == COLS - 1, 0.0, pltpu.roll(value, COLS - 1, 0))
    one, three = (right, left) if backward else (left, right)
    target[rows, 0:C] = one.astype(BF16)
    target[rows, C : 2 * C] = value.astype(BF16)
    target[rows, 2 * C : 3 * C] = three.astype(BF16)


def each_row(own, above, below, frames, ok, upcoming, target, make, backward):
    own_at, halo_at = (0, FR) if upcoming else (FR, 0)

    def put(source, i, frame, row, flag):
        value = make(source[chunk(i), :].astype(F32))
        if flag is not None:
            value = value * flag
        store_shifted(target, chunk(frame * (ROWS + 2) + row), value, backward)

    def inner(i, _):
        put(own, i, own_at + i // ROWS, i % ROWS + 1, None)
        return 0

    def edge(i, _):
        put(above, i, own_at + i, 0, ok[1])
        put(below, i, own_at + i, ROWS + 1, ok[2])
        return 0

    def outer(i, _):
        row = i % (ROWS + 2)
        flag = ok[0] * jnp.where(row == 0, ok[1], jnp.where(row == ROWS + 1, ok[2], 1.0))
        put(frames[0], i, halo_at + i // (ROWS + 2), row, flag)
        return 0

    def outer_inner(i, _):
        put(frames[0], i, halo_at + i // ROWS, i % ROWS + 1, ok[0])
        return 0

    def outer_edge(i, _):
        put(frames[1], i, halo_at + i, 0, ok[0] * ok[1])
        put(frames[2], i, halo_at + i, ROWS + 1, ok[0] * ok[2])
        return 0

    lax.fori_loop(0, FR * ROWS, inner, 0, unroll=2)
    lax.fori_loop(0, FR, edge, 0, unroll=2)
    if len(frames) == 1:
        lax.fori_loop(0, FR * (ROWS + 2), outer, 0, unroll=2)
    else:
        lax.fori_loop(0, FR * ROWS, outer_inner, 0)
        lax.fori_loop(0, FR, outer_edge, 0)


def conv(patches, weight, write, backward):
    for t in range(FR):
        total = None
        for a in range(3):
            for b in range(3):
                f, r = (t + 2 - a, 2 - b) if backward else (t + a, b)
                at = (f * (ROWS + 2) + r) * COLS
                left = patches[at : at + BAND, :]
                tap = (9 * a + 3 * b) * C
                if backward:
                    right = jnp.concatenate([weight[tap + k * C : tap + (k + 1) * C, :] for k in range(3)], axis=1)
                    part = lax.dot_general(left, right, (((1,), (1,)), ((), ())), preferred_element_type=F32)
                else:
                    part = jnp.dot(left, weight[tap : tap + 3 * C, :], preferred_element_type=F32)
                total = part if total is None else total + part
        write(t, total * SCALE)


def both_frames(patches, place):
    starts = [(f * (ROWS + 2) + r) * COLS for f, r in map(place, range(FR))]
    return jnp.concatenate([patches[at : at + BAND, :] for at in starts], axis=0)


def cut_blocks(blocks, whole, core, kept, given):
    for i in blocks:
        for side, outs in ((1 - core, given), (core, kept)):
            at = pl.multiple_of(i * BLOCK + side * (BLOCK // 2), 8)
            slab = whole[pl.ds(at, BLOCK // 2 + 8), :]
            for x in range(4):
                rows = slab[x * (SHARE // 2) : x * (SHARE // 2) + PIECE // 2, :]
                piece = jnp.concatenate([rows[:, :128], rows[:, 128:]], axis=0)
                outs[i // 4].ref[i % 4 * 4 + x] = piece.astype(BF16)
            if i % 4 == 3:
                outs[i // 4].send()


def wgrad(product, whole, core, kept, given):
    done = 0
    whole[27 * C :, :] = jnp.zeros((8, C), F32)
    for a in range(3):
        for b in range(3):
            tap = (9 * a + 3 * b) * C
            product(a, b, whole.at[tap : tap + 3 * C, :])
            ready = (tap + 3 * C) // BLOCK
            cut_blocks(range(done, ready), whole, core, kept, given)
            done = ready


def silu_parts(value, center, inverse, gain):
    hat = (value - center) * inverse
    pre = hat * gain
    return hat, pre, jax.nn.sigmoid(pre)


def stats_kernel(inputs, row):
    inputs = inputs.get()
    row.ref[...] = local_moments(lambda i: inputs[chunk(i), :].astype(F32), FR * ROWS)


def conv_kernel(ok, inputs, above, below, frames, table, gain, weight, patches, middle, row):
    center, inverse = read_norm(table.get()[...])
    gain = gain.get()[...]

    def hidden(value):
        _, pre, gate = silu_parts(value, center, inverse, gain)
        return pre * gate

    each_row(inputs.get(), above.get(), below.get(), (frames.get(),), ok, False, patches.ref, hidden, False)
    patches.send()

    def write(t, value):
        middle.ref[t * BAND : (t + 1) * BAND, :] = value.astype(BF16)

    conv(patches.ref, weight.get(), write, False)
    middle.send()
    row.ref[...] = local_moments(lambda i: middle.ref[chunk(i), :].astype(F32), FR * ROWS)


def slopes(read, back, center, inverse, gain, slope, hidden=None):
    def step(i, sums):
        hat, pre, gate = silu_parts(read(i), center, inverse, gain)
        if hidden is not None:
            hidden[chunk(i), :] = (pre * gate).astype(BF16)
        here = back[chunk(i), :] * gate * (1.0 + pre * (1.0 - gate)) * gain
        slope[chunk(i), :] = here
        return sums[0] + folded(here), sums[1] + folded(here * hat)

    zero = jnp.zeros((8, C), F32)
    plain, cross = lax.fori_loop(0, FR * ROWS, step, (zero, zero), unroll=2)
    return pack_row(jnp.sum(plain, axis=0, keepdims=True), jnp.sum(cross, axis=0, keepdims=True))


def back_two_kernel(ok, cotangent, above, below, frames, weight, back, patches):
    each_row(
        cotangent.get(), above.get(), below.get(), (frames.get(),), ok, True, patches.ref, lambda v: v, True
    )
    patches.send()

    def write(t, value):
        back.ref[t * BAND : (t + 1) * BAND, :] = value

    conv(patches.ref, weight.get(), write, True)


def second_kernel(core, middle, back, patches, table, gain, slope, row, *refs):
    kept, given, (hidden, whole) = refs[:4], refs[4:8], refs[8:]
    center, inverse = read_norm(table.get()[...])
    middle = middle.get()
    read = lambda i: middle[chunk(i), :].astype(F32)
    row.ref[...] = slopes(read, back.get(), center, inverse, gain.get()[...], slope.ref, hidden)
    slope.send()
    turned = hidden[...].astype(F32).T.astype(BF16)
    patches = patches.get()

    def product(a, b, rows):
        right = both_frames(patches, lambda t: (t + 2 - a, 2 - b))
        total = jnp.dot(turned, right, preferred_element_type=F32) * SCALE
        for c in range(3):
            rows[c * C : (c + 1) * C, :] = total[:, c * C : (c + 1) * C]

    wgrad(product, whole, core[0], kept, given)


def grad_one_kernel(core, slope, middle, patches, table, sums, mid_grad, *refs):
    kept, given, (whole,) = refs[:4], refs[4:8], refs[8:]
    center, inverse = read_norm(table.get()[...])
    mean, cross = read_sums(sums.get()[...])
    slope, middle = slope.get(), middle.get()

    def step(i, _):
        hat = (middle[chunk(i), :].astype(F32) - center) * inverse
        mid_grad.ref[chunk(i), :] = (inverse * (slope[chunk(i), :] - mean - hat * cross)).astype(BF16)
        return 0

    lax.fori_loop(0, FR * ROWS, step, 0, unroll=2)
    mid_grad.send()

    def product(a, b, rows):
        left = both_frames(patches.get(a + FR - 1), lambda t: (t + a, b))
        grad = mid_grad.ref[...]
        total = lax.dot_general(left, grad, (((0,), (0,)), ((), ())), preferred_element_type=F32)
        rows[...] = total * SCALE

    wgrad(product, whole, core[0], kept, given)


def back_one_kernel(
    ok, mid_grad, above, below, frames, above_frames, below_frames, weight, inputs, table, gain, slope, row, patches, back
):
    beyond = (frames.get(), above_frames.get(), below_frames.get())
    each_row(mid_grad.get(), above.get(), below.get(), beyond, ok, True, patches, lambda v: v, True)

    def write(t, value):
        back[t * BAND : (t + 1) * BAND, :] = value

    conv(patches, weight.get(), write, True)
    center, inverse = read_norm(table.get()[...])
    inputs = inputs.get()
    read = lambda i: inputs[chunk(i), :].astype(F32)
    row.ref[...] = slopes(read, back, center, inverse, gain.get()[...], slope.ref)[: row.ref.shape[0]]


def last_kernel(core, band, *refs):
    lines, (slope, inputs, table, cotangent, weight, result, flat, halves, arrive) = refs[:8], refs[8:]
    copies = []
    for n in range(2):
        place = core[0] if n == 0 else 1 - core[0]
        for k in range(4):
            x = lax.rem(band[0] - k + 4, 4)
            copies.append(pltpu.make_async_copy(lines[4 * n + k], halves.at[place, x], arrive.at[n, k]))
            copies[-1].start()
    center, inverse = read_norm(table.get()[...])
    for copy in copies:
        copy.wait()

    def block(i, _):
        assemble(i, lambda s: halves[s // 4, s % 4, i], weight.ref, flat)
        return 0

    for k in range(4):
        lax.fori_loop(4 * k, 4 * k + 4, block, 0)
        weight.send(k)

    def add(i, sums):
        for k in range(8):
            piece = halves[k // 4, k % 4, i, 48:, :].astype(F32)
            sums = sums + piece[:8] + piece[56:]
        return sums

    sums = lax.fori_loop(0, 16, add, jnp.zeros((8, 128), F32))
    mean, cross = read_sums(sums[6:])
    slope, inputs, cotangent = slope.get(), inputs.get(), cotangent.get()

    def step(i, _):
        hat = (inputs[chunk(i), :].astype(F32) - center) * inverse
        grad = inverse * (slope[chunk(i), :] - mean - hat * cross)
        result.ref[chunk(i), :] = (cotangent[chunk(i), :].astype(F32) + grad).astype(BF16)
        return 0

    lax.fori_loop(0, FR * ROWS, step, 0, unroll=2)


def adam_step(arrived, own, first, second, first_new, second_new, extra, flat):
    gradient = jnp.zeros((PIECE, 128), F32)
    for k in range(4):
        ready = arrived.get(k)
        gradient = lax.fori_loop(16 * k, 16 * k + 16, lambda i, s: s + ready[i].astype(F32), gradient)
    flat[pl.ds(0, PIECE // 2, 2), :] = gradient[: PIECE // 2]
    flat[pl.ds(1, PIECE // 2, 2), :] = gradient[PIECE // 2 :]
    gradient = flat[:SHARE, :]
    one = beta_one * first.get()[...] + (1.0 - beta_one) * gradient
    two = beta_two * second.get()[...] + (1.0 - beta_two) * gradient * gradient
    first_new.ref[...] = one
    second_new.ref[...] = two
    updated = own.get()[...].astype(F32) * (1.0 - learn_rate * decay_rate) - learn_rate * (one / first_fix) / (
        jnp.sqrt(two / second_fix) + adam_eps
    )
    flat[...] = jnp.concatenate([updated, extra], axis=0)
    halves = [flat[pl.ds(n, PIECE // 2, 2), :] for n in range(2)]
    return jnp.concatenate(halves, axis=0).astype(BF16)


def adam_two_kernel(arrived, own, first, second, first_new, second_new, part, flat):
    extra = jnp.zeros((PIECE - SHARE, 128), F32)
    part.ref[0] = adam_step(arrived, own, first, second, first_new, second_new, extra, flat)


def adam_one_kernel(arrived, own, first, second, sums, first_new, second_new, spread, flat):
    rest = sums.get()[0:1, :]
    terms = []
    for _ in range(3):
        terms.append(rest.astype(BF16).astype(F32))
        rest = rest - terms[-1]
    extra = jnp.concatenate([*terms, jnp.zeros((1, 128), F32)], axis=0)
    piece = adam_step(arrived, own, first, second, first_new, second_new, extra, flat)

    def copy(i, _):
        spread.ref[i] = piece
        return 0

    lax.fori_loop(0, spread.ref.shape[0], copy, 0)


def assemble(block, piece, weight, wide):
    for s in range(8):
        share = piece(s).astype(F32)
        rows = slice(s * (SHARE // 2), s * (SHARE // 2) + PIECE // 2)
        wide[rows, :128] = share[: PIECE // 2]
        wide[rows, 128:] = share[PIECE // 2 :]
    rows = pl.ds(pl.multiple_of(block * BLOCK, BLOCK), BLOCK)
    weight[rows, :] = wide[:BLOCK, :].astype(BF16)


def assemble_kernel(core, own, other, weight, flat, halves, arrive):
    parts = 4
    copies = [
        [
            pltpu.make_async_copy(
                source.at[pl.ds(16 * k, 16)], halves.at[place, pl.ds(16 * k, 16)], arrive.at[n, k]
            )
            for n, (source, place) in enumerate(((own, core[0]), (other, 1 - core[0])))
        ]
        for k in range(parts)
    ]
    for pair in copies:
        for copy in pair:
            copy.start()
    for k in range(parts):
        for copy in copies[k]:
            copy.wait()

        def block(i, _):
            assemble(i, lambda s: halves[s // 4, i * 4 + s % 4], weight.ref, flat)
            return 0

        lax.fori_loop(4 * k, 4 * k + 4, block, 0)
        weight.send(k)


class Coming:
    def __init__(self, ref, copies=()):
        self.ref, self.copies = ref, list(copies)
        for copy in self.copies:
            copy.start()
        self.parts = len(self.copies)

    def get(self, part=None):
        last = self.parts - 1 if part is None else part
        while self.copies and self.parts - len(self.copies) <= last:
            self.copies.pop(0).wait()
        return self.ref


class Going:
    def __init__(self, ref, copies=()):
        self.ref, self.copies, self.sent = ref, list(copies), set()

    def send(self, part=None):
        for k in range(len(self.copies)) if part is None else (part,):
            if k not in self.sent:
                self.copies[k].start()
                self.sent.add(k)

    def finish(self):
        self.send()
        for copy in self.copies:
            copy.wait()


SMALL, SMALL_RESULT = 16 * 1024, 80 * 1024


def run(kernel, scalars, arrays, outs, scratch=(), mib=60, parts=(), raw=()):
    parts, count = dict(parts), len(arrays)
    vmem, hbm = pl.BlockSpec(memory_space=pltpu.VMEM), pl.BlockSpec(memory_space=pl.ANY)
    every = [*arrays, *outs]
    large = [x.size * x.dtype.itemsize > (SMALL if n < count else SMALL_RESULT) for n, x in enumerate(every)]
    staged = [n for n in range(len(every)) if large[n] and n not in raw]
    buffers = [pltpu.VMEM(every[n].shape, every[n].dtype) for n in staged]
    semaphores = [pltpu.SemaphoreType.DMA((parts.get(n, 1),)) for n in staged]

    def body(*refs):
        lead, rest = refs[: len(scalars)], refs[len(scalars) :]
        places, rest = rest[: len(every)], rest[len(every) :]
        own, rest = rest[: len(scratch)], rest[len(scratch) :]
        boxes = [None] * len(every)
        for n in sorted(range(len(every)), key=lambda n: every[n].size > 128 * 128):
            place, kind = places[n], Coming if n < count else Going
            if n in raw:
                boxes[n] = place
                continue
            if not large[n]:
                boxes[n] = kind(place)
                continue
            at = staged.index(n)
            buffer, arrive, cuts = rest[at], rest[len(staged) + at], parts.get(n, 1)
            size = every[n].shape[0] // cuts
            copies = []
            for k in range(cuts):
                ends = [place.at[pl.ds(k * size, size)], buffer.at[pl.ds(k * size, size)]]
                source, target = ends if n < count else ends[::-1]
                copies.append(pltpu.make_async_copy(source, target, arrive.at[k]))
            boxes[n] = kind(buffer, copies)
        kernel(*lead, *boxes, *own)
        for n, box in enumerate(boxes):
            if n not in raw:
                box.get() if n < count else box.finish()

    return pl.pallas_call(
        body,
        out_shape=tuple(jax.ShapeDtypeStruct(x.shape, x.dtype) for x in outs),
        in_specs=[pl.BlockSpec(memory_space=pltpu.SMEM)] * len(scalars)
        + [hbm if large[n] else vmem for n in range(count)],
        out_specs=tuple(hbm if large[n] else vmem for n in range(count, len(every))),
        scratch_shapes=[*scratch, *buffers, *semaphores],
        compiler_params=pltpu.CompilerParams(vmem_limit_bytes=mib * 1024 * 1024),
        cost_estimate=pl.CostEstimate(flops=1024, bytes_accessed=1024, transcendentals=0),
    )(*scalars, *arrays)


def everyone(row):
    return lax.all_to_all(row, BOTH, 0, 0, tiled=True)


def after(value, *others):
    return lax.optimization_barrier((value, *others))[0]


def neighbours(axis):
    forward = [(i, i + 1) for i in range(lax.axis_size(axis) - 1)]
    return forward, [(j, i) for i, j in forward]


def edge_rows(last, leading, blocks):
    down, up = neighbours("rows")
    above, below = lax.ppermute(last, "rows", down), lax.ppermute(leading, "rows", up)
    return [(above[k : k + FR], below[k : k + FR]) for k in range(0, FR * blocks, FR)]


def five_sides(block):
    bands, steps = lax.axis_size("rows"), lax.axis_size("tm")
    last, leading = block[:, ROWS - 1], block[:, 0]
    _, backward = neighbours("tm")
    frames = lax.ppermute(block, "tm", backward)
    place = lambda t, r: t * bands + r
    falls = [(place(t, r), place(t - 1, r + 1)) for t in range(1, steps) for r in range(bands - 1)]
    rises = [(place(t, r), place(t - 1, r - 1)) for t in range(1, steps) for r in range(1, bands)]
    corners = lax.ppermute(last, BOTH, falls), lax.ppermute(leading, BOTH, rises)
    return ((frames, *corners), *edge_rows(last, leading, 1)[0])


def join_edges(block, edges):
    return jnp.concatenate([edges[0][:, None], block, edges[1][:, None]], axis=1)


def frame_halo(block, edges, perm):
    return lax.ppermute(join_edges(block, edges), "tm", perm).reshape(-1, C)


def flat(edges):
    return [edge.reshape(-1, C) for edge in edges]


def over_plane(pieces):
    return lax.all_to_all(pieces, BOTH, 0, 0, axis_index_groups=PLANE_GROUPS, tiled=True)


def over_line(piece):
    bands = lax.axis_size("rows")
    return [
        lax.ppermute(piece, "rows", [(i, (i + k) % bands) for i in range(bands)]) for k in range(1, bands)
    ]


def over_bands(piece):
    bands, here = lax.axis_size("rows"), lax.axis_index("rows")
    turned = [piece, *over_line(piece)]
    ordered = []
    for band in range(bands):
        choice = turned[0]
        for k in range(1, bands):
            choice = jnp.where((here - band) % bands == k, turned[k], choice)
        ordered.append(choice)
    return jnp.concatenate(ordered, axis=0)


def cells(array):
    return array.reshape(FR, ROWS, COLS, C)


def pair_kernel(*refs):
    kept, taken, result = refs[:4], refs[4:8], refs[8]
    for k in range(4):
        first, second = kept[k].get(), taken[k].get()
        for i in range(16):
            result.ref[16 * k + i] = (first[i].astype(F32) + second[i].astype(F32)).astype(BF16)
        result.send(k)


def pair_sum(kept, given):
    taken = [lax.ppermute(part, BOTH, CORE_PAIRS) for part in given]
    whole = jax.ShapeDtypeStruct((64, PIECE, 128), BF16)
    (total,) = run(pair_kernel, (), (*kept, *taken), (whole,), parts={8: 4}, mib=63)
    return total


def over_chips(pieces):
    return lax.all_to_all(pieces, BOTH, 0, 0, axis_index_groups=CHIP_GROUPS, tiled=True)


def own_share(weight):
    place = lax.axis_index(BOTH) * (SHARE // 2)
    return lax.dynamic_slice_in_dim(weight, place, SHARE // 2, axis=0).reshape(SHARE, 128)


def local(
    inputs,
    cotangent,
    gain_one,
    gain_two,
    weight_one,
    weight_two,
    first_one,
    second_one,
    first_two,
    second_two,
):
    shape = jax.ShapeDtypeStruct
    step, band = lax.axis_index("tm"), lax.axis_index("rows")
    core = (step % 2).astype(jnp.int32).reshape(1)
    inside = lambda *tests: jnp.stack([jnp.where(t, 1.0, 0.0).astype(F32) for t in tests])
    above_ok, below_ok = band > 0, band < lax.axis_size("rows") - 1
    ok_before = inside(step > 0, above_ok, below_ok)
    ok_after = inside(step < lax.axis_size("tm") - 1, above_ok, below_ok)
    gain_one, gain_two = gain_one.reshape(1, C), gain_two.reshape(1, C)
    flat_inputs, flat_cot = inputs.reshape(CELLS, C), cotangent.reshape(CELLS, C)

    row_type = shape((128, 128), F32)
    act_type, wide_type = shape((CELLS, C), BF16), shape((CELLS, C), F32)
    patch_type = shape((EXT, 3 * C), BF16)
    piece_types = (shape((16, PIECE, 128), BF16),) * 8
    moment_type = shape((SHARE, 128), F32)
    patch_scratch = pltpu.VMEM((EXT, 3 * C), BF16)
    whole_scratch = pltpu.VMEM((27 * C + 8, C), F32)

    def update(kernel, arrived, weight, first, second, more, part_types):
        first_new, second_new, *part = run(
            kernel,
            (),
            (*arrived, own_share(weight), first.reshape(SHARE, 128), second.reshape(SHARE, 128), *more),
            (moment_type, moment_type, *part_types),
            (pltpu.VMEM((PIECE, 128), F32),),
            parts={0: 4},
            mib=16,
        )
        return part, first_new.reshape(-1), second_new.reshape(-1)

    forward, backward = neighbours("tm")
    first_edges = [
        jnp.concatenate([block[:, at] for block in (inputs, cotangent)], axis=0) for at in (ROWS - 1, 0)
    ]
    edges_in, edges_cot = edge_rows(*first_edges, 2)
    (row_one,) = run(stats_kernel, (), (flat_inputs,), (row_type,))
    frames_in = frame_halo(after(inputs, row_one), edges_in, forward)
    frames_cot = frame_halo(after(cotangent, row_one), edges_cot, backward)
    table_one = everyone(row_one)
    patch_one, middle, row_two = run(
        conv_kernel,
        (ok_before,),
        (flat_inputs, *flat(edges_in), frames_in, table_one, gain_one, weight_one),
        (patch_type, act_type, row_type),
    )
    table_two = everyone(row_two)
    back_two, patch_cot = run(
        back_two_kernel,
        (ok_after,),
        (after(flat_cot, row_two), *flat(edges_cot), frames_cot, weight_two),
        (wide_type, patch_type),
    )
    slope_two, row_three, *cuts_two = run(
        second_kernel,
        (core,),
        (middle, back_two, patch_cot, table_two, gain_two),
        (wide_type, row_type, *piece_types),
        (pltpu.VMEM((CELLS, C), BF16), whole_scratch),
        parts={2: 4},
    )
    table_three = everyone(row_three)
    pair_two = pair_sum(cuts_two[:4], cuts_two[4:])
    mid_grad, *cuts_one = run(
        grad_one_kernel,
        (core,),
        (after(slope_two, pair_two), middle, patch_one, table_two, table_three),
        (act_type, *piece_types),
        (whole_scratch,),
        parts={2: 4},
    )
    frames_grad, *edges_grad = five_sides(cells(mid_grad))
    arrived_two = over_chips(pair_two)
    kept_first = after(cuts_one[0], *frames_grad, *edges_grad)
    pair_one = pair_sum((kept_first, *cuts_one[1:4]), cuts_one[4:])
    part_two, new_first_two, new_second_two = update(
        adam_two_kernel,
        (after(arrived_two, pair_one),),
        weight_two,
        first_two,
        second_two,
        (),
        (shape((1, PIECE, 128), BF16),),
    )
    arrived_one = over_chips(pair_one)
    line_two = over_bands(part_two[0])
    spread_two = jnp.broadcast_to(line_two.reshape(1, 4 * PIECE, 128), (16, 4 * PIECE, 128))
    slope_one, row_four = run(
        back_one_kernel,
        (ok_after,),
        (
            after(mid_grad, pair_one),
            *flat(edges_grad),
            *flat(frames_grad),
            weight_one,
            flat_inputs,
            table_one,
            gain_one,
        ),
        (wide_type, shape((8, 128), F32)),
        (patch_scratch, pltpu.VMEM((CELLS, C), F32)),
    )
    (part_one,), new_first_one, new_second_one = update(
        adam_one_kernel,
        (after(arrived_one, line_two),),
        weight_one,
        first_one,
        second_one,
        (row_four,),
        (shape((16, PIECE, 128), BF16),),
    )
    own_one = over_plane(part_one)
    lines_one = [own_one, *over_line(own_one)]
    own_two = over_plane(after(spread_two, own_one))
    own_two = after(own_two, *lines_one)
    other_two = lax.ppermute(own_two, BOTH, CORE_PAIRS).reshape(64, PIECE, 128)
    others_one = [lax.ppermute(line, BOTH, CORE_PAIRS) for line in lines_one]
    weight_type = shape((27 * C, C), BF16)
    assemble_scratch = pltpu.VMEM((BLOCK + 8, C), F32)
    (new_weight_two,) = run(
        assemble_kernel,
        (core,),
        (own_two.reshape(64, PIECE, 128), other_two),
        (weight_type,),
        (assemble_scratch, pltpu.VMEM((2, 64, PIECE, 128), BF16), pltpu.SemaphoreType.DMA((2, 4))),
        mib=16,
        parts={2: 4},
        raw=(0, 1),
    )
    new_weight_one, input_grad = run(
        last_kernel,
        (core, band.astype(jnp.int32).reshape(1)),
        (*lines_one, *others_one, after(slope_one, new_weight_two), flat_inputs, table_one, flat_cot),
        (weight_type, act_type),
        (assemble_scratch, pltpu.VMEM((2, 4, 16, PIECE, 128), BF16), pltpu.SemaphoreType.DMA((2, 4))),
        mib=24,
        parts={12: 4},
        raw=range(8),
    )
    return (
        cells(input_grad),
        new_weight_one,
        new_weight_two,
        new_first_one,
        new_second_one,
        new_first_two,
        new_second_two,
    )


def solution(mesh):
    split, share = P("tm", "rows", None, None), P(("tm", "rows"))
    return jax.shard_map(
        local,
        mesh=mesh,
        in_specs=(split, split, P(), P(), P(), P(), share, share, share, share),
        out_specs=(split, P(), P(), share, share, share, share),
        check_vma=False,
    )
```
